32 devices in a mesh: dp: 4 (over y, x), tensor: 8 (over z, core).
Axes of the slice: x: 2, y: 2, z: 4, core: 2. Of those that a mesh axis runs over, the one named last changes fastest.
Arguments:
- inputs: bfloat16 [512, 4096], P('dp', 'tensor'), may hold values from -6 to 6
- cotangent: bfloat16 [512, 4096], P('dp', 'tensor'), may hold values from -6 to 6
- gate_w: bfloat16 [8, 96, 128, 128], P('tensor'), may hold values from -0.25 to 0.25
- up_w: bfloat16 [8, 96, 128, 128], P('tensor'), may hold values from -0.25 to 0.25
- down_w: bfloat16 [8, 96, 128, 128], P('tensor'), may hold values from -0.25 to 0.25
- gate_list: int32 [8, 96], P('tensor'), may hold values from -1 to 511, as said below
- up_list: int32 [8, 96], P('tensor'), may hold values from -1 to 511, as said below
- down_list: int32 [8, 96], P('tensor'), may hold values from -1 to 511, as said below
Outputs:
- grad_x: bfloat16 [512, 4096], P('dp', 'tensor')
- grad_gate_w: bfloat16 [8, 96, 128, 128], P('tensor', None, 'dp')
- grad_up_w: bfloat16 [8, 96, 128, 128], P('tensor', None, 'dp')
- grad_down_w: bfloat16 [8, 96, 128, 128], P('tensor', None, 'dp')
The draws below stay inside these ranges and needn't reach their ends.
Inputs may be any that keep to these rules, and one draw needn't show every extreme that they name: `gate_list`: row j of the list names blocks of hidden blocks j * 16 to j * 16 + 15 only; no entry appears twice in a row; live entries come first and -1 fills the rest; a row holds at most 96 live entries and some row holds exactly 96. `up_list`: as for gate_list, drawn independently. `down_list`: as for gate_list, drawn independently.
All inputs are finite; a program needn't handle non-finite values.
Results may differ from the reference program's by a relative error of at most 0.014.
Values may be sent and summed in bfloat16 or wider, within the bound.
A program may use at most 128 MiB of HBM per device.

```python
import math
import jax
import jax.numpy as jnp
from jax import lax

D = 4096
BLOCK = 128
TOK = 128
HB = 16
DB = 32
NBLK = 96
TOKENS = 512
N_DP = 4
N_TENSOR = 8


def make_list(key, salt):
    key = jax.random.fold_in(key, salt)
    key_count, key_top, key_pick = jax.random.split(key, 3)
    counts = jax.random.randint(key_count, (N_TENSOR,), NBLK // 3, NBLK + 1)
    chosen = jax.random.randint(key_top, (), 0, N_TENSOR)
    counts = jnp.where(jnp.arange(N_TENSOR) == chosen, NBLK, counts)
    slots = jnp.arange(NBLK)
    filler = HB * DB

    def pick_row(subkey, row_total):
        picked = jax.random.permutation(subkey, HB * DB)[:NBLK]
        kept = jnp.where(slots < row_total, picked, filler)
        ordered = jnp.sort(kept)
        return jnp.where(ordered == filler, -1, ordered)
    rows_all = jax.vmap(pick_row)(jax.random.split(key_pick, N_TENSOR), counts)
    return rows_all.astype(jnp.int32)


def draw_gate_list(key, part):
    return make_list(key, 11)


def draw_up_list(key, part):
    return make_list(key, 23)


def draw_down_list(key, part):
    return make_list(key, 37)


def shard_levels(key, dims, cuts, smallest, high):
    gain, own = 1.0, jax.random.fold_in(key, 6)
    for axis_at, parts in cuts:
        heights = jnp.exp(jax.random.uniform(jax.random.fold_in(own, axis_at), (parts,), jnp.float32, smallest / len(cuts), high / len(cuts)))
        gain = gain * jnp.repeat(heights, dims[axis_at] // parts).reshape([-1 if axis == axis_at else 1 for axis in range(len(dims))])
    return gain


def normal_values(own_key, shape, width, most, cuts=(), kind=jnp.bfloat16):
    loudness = shard_levels(own_key, shape, cuts, -0.22, 0.18) if cuts else 1.0
    result = jax.random.normal(own_key, shape, jnp.float32) * width * loudness
    return jnp.minimum(jnp.maximum(result, -most), most).astype(kind)


def setup_inputs(seed: int = 0) -> dict:
    streams_of = jax.random.split(jax.random.key(seed), 9)
    inputs = normal_values(streams_of[0], (TOKENS, D), 1.0, 6.0, ((0, 4), (1, 8)))
    cotangent = normal_values(streams_of[1], (TOKENS, D), 1.0, 6.0, ((0, 4), (1, 8)))
    gate_w = normal_values(streams_of[2], (N_TENSOR, NBLK, BLOCK, BLOCK), (D // 8) ** -0.5, 0.25, ((0, 8),))
    up_w = normal_values(streams_of[3], (N_TENSOR, NBLK, BLOCK, BLOCK), (D // 8) ** -0.5, 0.25, ((0, 8),))
    down_w = normal_values(streams_of[4], (N_TENSOR, NBLK, BLOCK, BLOCK), (D // 8) ** -0.5, 0.25, ((0, 8),))
    gate_list = draw_gate_list(jax.random.fold_in(streams_of[8], 71), 0)
    up_list = draw_up_list(jax.random.fold_in(streams_of[8], 71), 0)
    down_list = draw_down_list(jax.random.fold_in(streams_of[8], 71), 0)
    return {"inputs": inputs, "cotangent": cotangent, "gate_w": gate_w, "up_w": up_w, "down_w": down_w, "gate_list": gate_list, "up_list": up_list, "down_list": down_list}


def decode(entries, row_count):
    living = entries >= 0
    clamped = jnp.maximum(entries, 0)
    return (living, clamped // row_count, clamped % row_count)

def one_hot(block_index, width_count, living):
    return ((block_index[:, None] == jnp.arange(width_count)[None, :]) & living[:, None]).astype(jnp.float32)

def weight_term(products, grad_scale, living):
    rounded = (products * grad_scale).astype(jnp.bfloat16)
    rounded = lax.optimization_barrier(rounded)
    summed = lax.optimization_barrier(jnp.sum(rounded.astype(jnp.float32), axis=0))
    return (summed * living[:, None, None].astype(jnp.float32)).astype(jnp.bfloat16)

def reference(inputs, cotangent, gate_w, up_w, down_w, gate_list, up_list, down_list):
    highest = lax.Precision.HIGHEST
    grad_scale = 1.0 / math.sqrt(TOKENS)
    input_blocks = inputs.reshape(N_DP, TOK, DB, BLOCK)
    cot_blocks = cotangent.reshape(N_DP, TOK, DB, BLOCK)

    def owner(running, pieces):
        gate_blk, up_blk, down_blk, gate_ent, up_ent, down_ent = pieces
        gate_live, gate_feat, gate_row = decode(gate_ent, HB)
        up_live, up_feat, up_row = decode(up_ent, HB)
        down_live, down_feat, down_row = decode(down_ent, HB)
        gate_in = jnp.take(input_blocks, gate_feat, axis=2).astype(jnp.float32)
        up_in = jnp.take(input_blocks, up_feat, axis=2).astype(jnp.float32)
        gate_part = jnp.einsum('ptkc,kch->ptkh', gate_in, gate_blk.astype(jnp.float32))
        gate_val = jnp.einsum('ptkh,kr->ptrh', gate_part, one_hot(gate_row, HB, gate_live), precision=highest)
        up_part = jnp.einsum('ptkc,kch->ptkh', up_in, up_blk.astype(jnp.float32))
        up_val = jnp.einsum('ptkh,kr->ptrh', up_part, one_hot(up_row, HB, up_live), precision=highest)
        sigmoid_gate = jax.nn.sigmoid(gate_val)
        active = gate_val * sigmoid_gate
        hidden = (active * up_val).astype(jnp.bfloat16)
        down_cot = jnp.take(cot_blocks, down_feat, axis=2).astype(jnp.float32)
        hidden_down = jnp.take(hidden, down_row, axis=2).astype(jnp.float32)
        down_part = jnp.einsum('ptkc,khc->ptkh', down_cot, down_blk.astype(jnp.float32))
        grad_hidden = jnp.einsum('ptkh,kr->ptrh', down_part, one_hot(down_row, HB, down_live), precision=highest)
        down_grad = weight_term(jnp.einsum('ptkh,ptkc->pkhc', hidden_down, down_cot), grad_scale, down_live)
        grad_gate = (grad_hidden * up_val * sigmoid_gate * (1.0 + gate_val * (1.0 - sigmoid_gate))).astype(jnp.bfloat16)
        grad_up = (grad_hidden * active).astype(jnp.bfloat16)
        gate_back = jnp.take(grad_gate, gate_row, axis=2).astype(jnp.float32)
        up_back = jnp.take(grad_up, up_row, axis=2).astype(jnp.float32)
        gate_grad = weight_term(jnp.einsum('ptkc,ptkh->pkch', gate_in, gate_back), grad_scale, gate_live)
        up_grad = weight_term(jnp.einsum('ptkc,ptkh->pkch', up_in, up_back), grad_scale, up_live)
        back_gate = jnp.einsum('ptkh,kch->ptkc', gate_back, gate_blk.astype(jnp.float32))
        back_up = jnp.einsum('ptkh,kch->ptkc', up_back, up_blk.astype(jnp.float32))
        partial_sum = jnp.einsum('ptkc,kd->ptdc', back_gate, one_hot(gate_feat, DB, gate_live), precision=highest)
        partial_sum = partial_sum + jnp.einsum('ptkc,kd->ptdc', back_up, one_hot(up_feat, DB, up_live), precision=highest)
        rounded_sum = lax.optimization_barrier(partial_sum.astype(jnp.bfloat16))
        return (running + rounded_sum.astype(jnp.float32), (gate_grad, up_grad, down_grad))
    start_sum = jnp.zeros((N_DP, TOK, DB, BLOCK), jnp.float32)
    total, grads = lax.scan(owner, start_sum, (gate_w, up_w, down_w, gate_list, up_list, down_list))
    grad_x = total.reshape(TOKENS, D).astype(jnp.bfloat16)
    return (grad_x, grads[0], grads[1], grads[2])
```

```python
import functools
import math

import jax
import jax.numpy as jnp
from jax import lax
from jax.experimental import pallas as pl
from jax.experimental.pallas import tpu as pltpu
from jax.sharding import PartitionSpec as P

D = 4096
FF = 16384
BLOCK = 128
UNROLL = 2
BACK_UNROLL = 4
SLOT_UNROLL = 8
F32 = jnp.float32
BF16 = jnp.bfloat16


def decode(entries, row_count):
    living = entries >= 0
    clamped = jnp.maximum(entries, 0)
    return (living, clamped // row_count, clamped % row_count)


def one_hot(block_index, width_count, living):
    return ((block_index[:, None] == jnp.arange(width_count)[None, :]) & living[:, None]).astype(
        jnp.float32
    )


def select_sum(values, table):
    return jnp.sum(values[:, :, None, :] * table[None, :, :, None], axis=1)


def project_rows(blocks_in, weights, rows_hot):
    products = jnp.einsum("tkc,kch->tkh", blocks_in, weights, preferred_element_type=jnp.float32)
    return select_sum(products, rows_hot)


def weight_term(products, grad_scale, living):
    rounded = (products * grad_scale).astype(jnp.bfloat16)
    rounded = lax.optimization_barrier(rounded)
    return (rounded.astype(jnp.float32) * living[:, None, None].astype(jnp.float32))[None]


def add_sources(received):
    return jnp.sum(received.astype(jnp.float32), axis=1)


def plain_on_device(inputs, cotangent, gate_w, up_w, down_w, gate_list, up_list, down_list):
    tensor_size = lax.axis_size("tensor")
    hidden_rows = FF // (BLOCK * tensor_size)
    feat_blocks = D // BLOCK
    tokens_here = inputs.shape[0]
    grad_scale = 1.0 / math.sqrt(tokens_here * lax.axis_size("dp"))
    gate_live, gate_feat, gate_row = decode(gate_list[0], hidden_rows)
    up_live, up_feat, up_row = decode(up_list[0], hidden_rows)
    down_live, down_feat, down_row = decode(down_list[0], hidden_rows)
    whole_in, whole_cot = (
        lax.all_gather(inputs, "tensor", axis=1, tiled=True),
        lax.all_gather(cotangent, "tensor", axis=1, tiled=True),
    )
    input_blocks = whole_in.reshape(tokens_here, feat_blocks, BLOCK)
    gate_in = jnp.take(input_blocks, gate_feat, axis=1)
    up_in = jnp.take(input_blocks, up_feat, axis=1)
    gate_val = project_rows(gate_in, gate_w[0], one_hot(gate_row, hidden_rows, gate_live))
    up_val = project_rows(up_in, up_w[0], one_hot(up_row, hidden_rows, up_live))
    sigmoid_gate = jax.nn.sigmoid(gate_val)
    active = gate_val * sigmoid_gate
    hidden = (active * up_val).astype(jnp.bfloat16)
    cot_blocks = whole_cot.reshape(tokens_here, feat_blocks, BLOCK)
    down_cot = jnp.take(cot_blocks, down_feat, axis=1)
    hidden_down = jnp.take(hidden, down_row, axis=1)
    down_part = jnp.einsum("tkc,khc->tkh", down_cot, down_w[0], preferred_element_type=jnp.float32)
    grad_hidden = select_sum(down_part, one_hot(down_row, hidden_rows, down_live))
    down_term = weight_term(
        jnp.einsum("tkh,tkc->khc", hidden_down, down_cot, preferred_element_type=jnp.float32),
        grad_scale,
        down_live,
    )
    grad_gate = (
        grad_hidden * up_val * sigmoid_gate * (1.0 + gate_val * (1.0 - sigmoid_gate))
    ).astype(jnp.bfloat16)
    grad_up = (grad_hidden * active).astype(jnp.bfloat16)
    gate_back = jnp.take(grad_gate, gate_row, axis=1)
    up_back = jnp.take(grad_up, up_row, axis=1)
    gate_term = weight_term(
        jnp.einsum("tkc,tkh->kch", gate_in, gate_back, preferred_element_type=jnp.float32),
        grad_scale,
        gate_live,
    )
    up_term = weight_term(
        jnp.einsum("tkc,tkh->kch", up_in, up_back, preferred_element_type=jnp.float32),
        grad_scale,
        up_live,
    )
    back_gate = jnp.einsum("tkh,kch->tkc", gate_back, gate_w[0], preferred_element_type=jnp.float32)
    back_up = jnp.einsum("tkh,kch->tkc", up_back, up_w[0], preferred_element_type=jnp.float32)
    partial_sum = select_sum(back_gate, one_hot(gate_feat, feat_blocks, gate_live))
    partial_sum = partial_sum + select_sum(back_up, one_hot(up_feat, feat_blocks, up_live))
    pieces = partial_sum.astype(jnp.bfloat16).reshape(tokens_here, tensor_size, D // tensor_size)
    summed = add_sources(lax.all_to_all(pieces, "tensor", split_axis=1, concat_axis=1, tiled=True))
    grad_x = summed.astype(jnp.bfloat16)
    gate_sum, up_sum, down_sum = (
        lax.psum_scatter(
            gate_term.astype(jnp.bfloat16), "dp", scatter_dimension=2, tiled=True
        ).astype(jnp.float32),
        lax.psum_scatter(
            up_term.astype(jnp.bfloat16), "dp", scatter_dimension=2, tiled=True
        ).astype(jnp.float32),
        lax.psum_scatter(
            down_term.astype(jnp.bfloat16), "dp", scatter_dimension=2, tiled=True
        ).astype(jnp.float32),
    )
    return (
        grad_x,
        gate_sum.astype(jnp.bfloat16),
        up_sum.astype(jnp.bfloat16),
        down_sum.astype(jnp.bfloat16),
    )


def pair_tables(lists, hidden_rows, length):
    slots = lists.shape[1]
    live = lists >= 0
    clamped = jnp.maximum(lists, 0)
    feat, row = clamped // hidden_rows, clamped % hidden_rows
    hot = (row[:, :, None] == jnp.arange(hidden_rows)) & live[:, :, None]
    counts = jnp.sum(hot.astype(jnp.int32), axis=1)
    padded = (counts + 1) // 2 * 2
    order = jnp.arange(slots)
    same = (row[:, :, None] == row[:, None, :]) & (order[None, :] < order[:, None])
    rank = jnp.sum(same.astype(jnp.int32), axis=2)
    before = jnp.arange(hidden_rows) < row[:, :, None]
    start = jnp.sum(jnp.where(before, padded[:, None, :], 0), axis=2)
    place = jnp.where(live, start + rank, -1)
    here = place[:, :, None] == jnp.arange(length)
    slot = jnp.sum(jnp.where(here, (order - slots)[None, :, None], 0), axis=1) + slots
    feat_at = jnp.sum(jnp.where(here, feat[:, :, None], 0), axis=1)
    row_at = jnp.sum(jnp.where(here, row[:, :, None], 0), axis=1)
    pairs = jnp.sum(padded, axis=1) // 2
    living = jnp.sum(live.astype(jnp.int32), axis=1)
    return jnp.concatenate([slot, feat_at, row_at], axis=0), jnp.concatenate([pairs, living])


def nt_dot(a, b):
    return lax.dot_general(a, b, (((1,), (1,)), ((), ())), preferred_element_type=F32)


def layer_kernel(
    hidden_rows, feat_blocks, groups, tok, grad_scale,
    counts, tables, lists, in_hbm, cot_hbm, gate_hbm, up_hbm, down_hbm,
    part_ref, ggw_ref, guw_ref, gdw_ref,
    xin, cot, gw, uw, dw, gate, up, gh, gg, gu, hid, xt, ht, dense, back_g, back_u, sems,
):
    slots = lists.shape[1]
    tokens = groups * tok
    rows = BLOCK // groups
    pick = groups
    me = lax.axis_index("dp")
    copies = [
        pltpu.make_async_copy(src, dst, sems.at[i])
        for i, (src, dst) in enumerate((
            (in_hbm, xin),
            (gate_hbm.at[0], gw.at[pl.ds(0, slots)]),
            (up_hbm.at[0], uw.at[pl.ds(0, slots)]),
            (cot_hbm, cot),
            (down_hbm.at[0], dw.at[pl.ds(0, slots)]),
        ))
    ]
    for copy in copies:
        copy.start()
    blank = jnp.zeros((BLOCK, BLOCK), BF16)
    gw[slots] = blank
    uw[slots] = blank
    dw[slots] = blank

    @pl.loop(0, hidden_rows)
    def _(h):
        zero = jnp.zeros((tokens, BLOCK), F32)
        gate[h] = zero
        up[h] = zero
        gh[h] = zero

    @pl.loop(0, feat_blocks)
    def _(d):
        zero = jnp.zeros((tok, BLOCK), F32)
        back_g[d] = zero
        back_u[d] = zero

    for copy in copies:
        copy.wait()

    pairs = jnp.maximum(jnp.maximum(counts[0], counts[1]), counts[2])

    @pl.loop(0, (pairs + UNROLL - 1) // UNROLL)
    def _(t):
        for u in range(UNROLL):
            a = 2 * (t * UNROLL + u)
            b = a + 1
            for i, (acts, w, acc) in enumerate(((xin, gw, gate), (xin, uw, up), (cot, dw, gh))):
                left = jnp.concatenate([acts[tables[3 + i, a]], acts[tables[3 + i, b]]], axis=1)
                one, two = w[tables[i, a]], w[tables[i, b]]
                h = tables[6 + i, a]
                if i < 2:
                    got = jnp.dot(
                        left, jnp.concatenate([one, two], axis=0), preferred_element_type=F32
                    )
                else:
                    got = nt_dot(left, jnp.concatenate([one, two], axis=1))
                acc[h] += got

    @pl.loop(0, hidden_rows)
    def _(h):
        @pl.loop(0, tokens // 128)
        def _(r):
            at = pl.ds(pl.multiple_of(r * 128, 128), 128)
            g, u, y = gate[h, at], up[h, at], gh[h, at]
            sig = 1.0 / (1.0 + jnp.exp(-g))
            act = g * sig
            hid[h, at] = (act * u).astype(BF16)
            gg[h, at] = (y * u * sig * (1.0 + g * (1.0 - sig))).astype(BF16)
            gu[h, at] = (y * act).astype(BF16)

    own = pl.ds(pl.multiple_of(me * tok, tok), tok)
    living = jnp.maximum(counts[3], counts[4])

    @pl.loop(0, (living + BACK_UNROLL - 1) // BACK_UNROLL)
    def _(t):
        for u in range(BACK_UNROLL):
            k = t * BACK_UNROLL + u
            for i, (grad, w, acc) in enumerate(((gg, gw, back_g), (gu, uw, back_u))):
                e = lists[i, k]
                block = w[jnp.where(e >= 0, k, slots)]
                e = jnp.maximum(e, 0)
                acc[e // hidden_rows] += nt_dot(grad[e % hidden_rows, own], block)

    @pl.loop(0, feat_blocks)
    def _(d):
        part_ref[d] = (back_g[d] + back_u[d]).astype(BF16)

    line = lax.broadcasted_iota(jnp.int32, (pick * BLOCK, BLOCK), 0)
    lane = lax.broadcasted_iota(jnp.int32, (pick * BLOCK, BLOCK), 1)
    want = (lane // rows) * BLOCK + me * rows + lane % rows
    chooser = jnp.where(line == want, 1.0, 0.0).astype(BF16)

    def own_rows(src, dst, count):
        @pl.loop(0, count // pick)
        def _(g):
            wide = jnp.concatenate([src[g * pick + q] for q in range(pick)], axis=1)
            chosen = jnp.dot(wide, chooser, preferred_element_type=F32)
            at = pl.ds(pl.multiple_of(g * BLOCK, BLOCK), BLOCK)
            dst[at, :] = chosen.T.astype(BF16)

    own_rows(xin, xt, feat_blocks)
    own_rows(hid, ht, hidden_rows)

    def all_products(left, right, count):
        @pl.loop(0, count // 2)
        def _(n):
            two = jnp.concatenate([right[2 * n], right[2 * n + 1]], axis=1)
            got = jnp.dot(left[...], two, preferred_element_type=F32) * grad_scale
            got = got.astype(BF16)
            per = left.shape[0] // rows
            for s in range(2):
                dense[pl.ds((2 * n + s) * per, per)] = got[:, s * BLOCK:(s + 1) * BLOCK].reshape(
                    per, rows, BLOCK
                )

    def keep_live(i, out, by_feat):
        @pl.loop(0, slots // SLOT_UNROLL)
        def _(t):
            for u in range(SLOT_UNROLL):
                k = t * SLOT_UNROLL + u
                e = lists[i, k]
                c = jnp.maximum(e, 0)
                d, h = c // hidden_rows, c % hidden_rows
                at = d * hidden_rows + h if by_feat else h * feat_blocks + d
                block = dense[at]
                out[0, k] = jnp.where(e >= 0, block, jnp.zeros_like(block))

    all_products(xt, gg, hidden_rows)
    keep_live(0, ggw_ref, False)
    all_products(xt, gu, hidden_rows)
    keep_live(1, guw_ref, False)
    all_products(ht, cot, feat_blocks)
    keep_live(2, gdw_ref, True)


def layer(whole_in, whole_cot, gate_w, up_w, down_w, lists, tables, counts, hidden_rows, groups):
    feat_blocks, tokens, _ = whole_in.shape
    slots = lists.shape[1]
    tok = tokens // groups
    rows = BLOCK // groups
    grad_scale = 1.0 / math.sqrt(tokens)
    smem = pl.BlockSpec(memory_space=pltpu.SMEM)
    vmem = pl.BlockSpec(memory_space=pltpu.VMEM)
    hbm = pl.BlockSpec(memory_space=pl.ANY)
    weights = pltpu.VMEM((slots + 1, BLOCK, BLOCK), BF16)
    acts = pltpu.VMEM((feat_blocks, tokens, BLOCK), BF16)
    wide = pltpu.VMEM((hidden_rows, tokens, BLOCK), F32)
    narrow = pltpu.VMEM((hidden_rows, tokens, BLOCK), BF16)
    grad = jax.ShapeDtypeStruct((1, slots, rows, BLOCK), BF16)
    back = pltpu.VMEM((feat_blocks, tok, BLOCK), F32)
    return pl.pallas_call(
        functools.partial(layer_kernel, hidden_rows, feat_blocks, groups, tok, grad_scale),
        out_shape=(jax.ShapeDtypeStruct((feat_blocks, tok, BLOCK), BF16), grad, grad, grad),
        in_specs=[smem, smem, smem, hbm, hbm, hbm, hbm, hbm],
        out_specs=[vmem] * 4,
        scratch_shapes=[
            acts, acts, weights, weights, weights, wide, wide, wide, narrow, narrow, narrow,
            pltpu.VMEM((feat_blocks * rows, tokens), BF16),
            pltpu.VMEM((hidden_rows * rows, tokens), BF16),
            pltpu.VMEM((feat_blocks * hidden_rows, rows, BLOCK), BF16),
            back, back,
            pltpu.SemaphoreType.DMA((5,)),
        ],
        compiler_params=pltpu.CompilerParams(vmem_limit_bytes=60 * 1024 * 1024),
        name="layer",
    )(counts, tables, lists, whole_in, whole_cot, gate_w, up_w, down_w)


def on_device(inputs, cotangent, gate_w, up_w, down_w, gate_list, up_list, down_list):
    tensor_size, groups = lax.axis_size("tensor"), lax.axis_size("dp")
    hidden_rows = FF // (BLOCK * tensor_size)
    tok, width = inputs.shape
    mine = width // BLOCK
    slots = gate_list.shape[1]
    lists = jnp.concatenate([gate_list, up_list, down_list], axis=0)
    step = 2 * UNROLL
    length = (slots + hidden_rows + step - 1) // step * step
    tables, counts = pair_tables(lists, hidden_rows, length)

    def whole(x):
        x = x.reshape(tok, mine, BLOCK).transpose(1, 0, 2)
        x = lax.all_gather(x, "tensor", axis=0, tiled=True)
        return lax.all_gather(x, "dp", axis=1, tiled=True)

    part, ggw, guw, gdw = layer(
        whole(inputs), whole(cotangent), gate_w, up_w, down_w, lists, tables, counts,
        hidden_rows, groups,
    )
    pieces = part.reshape(tensor_size, mine, tok, BLOCK)
    got = lax.all_to_all(pieces, "tensor", split_axis=0, concat_axis=0, tiled=True)
    summed = jnp.sum(got.astype(F32), axis=0).astype(BF16)
    grad_x = summed.transpose(1, 0, 2).reshape(tok, width)
    return grad_x, ggw, guw, gdw


def fits(mesh):
    return BLOCK // mesh.shape["dp"] >= 16


def solution(mesh):
    return jax.shard_map(
        on_device if fits(mesh) else plain_on_device,
        mesh=mesh,
        in_specs=(
            P("dp", "tensor"),
            P("dp", "tensor"),
            P("tensor", None, None, None),
            P("tensor", None, None, None),
            P("tensor", None, None, None),
            P("tensor", None),
            P("tensor", None),
            P("tensor", None),
        ),
        out_specs=(
            P("dp", "tensor"),
            P("tensor", None, "dp", None),
            P("tensor", None, "dp", None),
            P("tensor", None, "dp", None),
        ),
        check_vma=False,
    )
```

```python
import functools
import math

import jax
import jax.numpy as jnp
from jax import lax
from jax.experimental import pallas as pl
from jax.experimental.pallas import tpu as pltpu
from jax.sharding import PartitionSpec as P

D = 4096
FF = 16384
BLOCK = 128
UNROLL = 2
BACK_UNROLL = 4
SLOT_UNROLL = 8
F32 = jnp.float32
BF16 = jnp.bfloat16


def decode(entries, row_count):
    living = entries >= 0
    clamped = jnp.maximum(entries, 0)
    return (living, clamped // row_count, clamped % row_count)


def one_hot(block_index, width_count, living):
    return ((block_index[:, None] == jnp.arange(width_count)[None, :]) & living[:, None]).astype(
        jnp.float32
    )


def select_sum(values, table):
    return jnp.sum(values[:, :, None, :] * table[None, :, :, None], axis=1)


def project_rows(blocks_in, weights, rows_hot):
    products = jnp.einsum("tkc,kch->tkh", blocks_in, weights, preferred_element_type=jnp.float32)
    return select_sum(products, rows_hot)


def weight_term(products, grad_scale, living):
    rounded = (products * grad_scale).astype(jnp.bfloat16)
    rounded = lax.optimization_barrier(rounded)
    return (rounded.astype(jnp.float32) * living[:, None, None].astype(jnp.float32))[None]


def add_sources(received):
    return jnp.sum(received.astype(jnp.float32), axis=1)


def plain_on_device(inputs, cotangent, gate_w, up_w, down_w, gate_list, up_list, down_list):
    tensor_size = lax.axis_size("tensor")
    hidden_rows = FF // (BLOCK * tensor_size)
    feat_blocks = D // BLOCK
    tokens_here = inputs.shape[0]
    grad_scale = 1.0 / math.sqrt(tokens_here * lax.axis_size("dp"))
    gate_live, gate_feat, gate_row = decode(gate_list[0], hidden_rows)
    up_live, up_feat, up_row = decode(up_list[0], hidden_rows)
    down_live, down_feat, down_row = decode(down_list[0], hidden_rows)
    whole_in, whole_cot = (
        lax.all_gather(inputs, "tensor", axis=1, tiled=True),
        lax.all_gather(cotangent, "tensor", axis=1, tiled=True),
    )
    input_blocks = whole_in.reshape(tokens_here, feat_blocks, BLOCK)
    gate_in = jnp.take(input_blocks, gate_feat, axis=1)
    up_in = jnp.take(input_blocks, up_feat, axis=1)
    gate_val = project_rows(gate_in, gate_w[0], one_hot(gate_row, hidden_rows, gate_live))
    up_val = project_rows(up_in, up_w[0], one_hot(up_row, hidden_rows, up_live))
    sigmoid_gate = jax.nn.sigmoid(gate_val)
    active = gate_val * sigmoid_gate
    hidden = (active * up_val).astype(jnp.bfloat16)
    cot_blocks = whole_cot.reshape(tokens_here, feat_blocks, BLOCK)
    down_cot = jnp.take(cot_blocks, down_feat, axis=1)
    hidden_down = jnp.take(hidden, down_row, axis=1)
    down_part = jnp.einsum("tkc,khc->tkh", down_cot, down_w[0], preferred_element_type=jnp.float32)
    grad_hidden = select_sum(down_part, one_hot(down_row, hidden_rows, down_live))
    down_term = weight_term(
        jnp.einsum("tkh,tkc->khc", hidden_down, down_cot, preferred_element_type=jnp.float32),
        grad_scale,
        down_live,
    )
    grad_gate = (
        grad_hidden * up_val * sigmoid_gate * (1.0 + gate_val * (1.0 - sigmoid_gate))
    ).astype(jnp.bfloat16)
    grad_up = (grad_hidden * active).astype(jnp.bfloat16)
    gate_back = jnp.take(grad_gate, gate_row, axis=1)
    up_back = jnp.take(grad_up, up_row, axis=1)
    gate_term = weight_term(
        jnp.einsum("tkc,tkh->kch", gate_in, gate_back, preferred_element_type=jnp.float32),
        grad_scale,
        gate_live,
    )
    up_term = weight_term(
        jnp.einsum("tkc,tkh->kch", up_in, up_back, preferred_element_type=jnp.float32),
        grad_scale,
        up_live,
    )
    back_gate = jnp.einsum("tkh,kch->tkc", gate_back, gate_w[0], preferred_element_type=jnp.float32)
    back_up = jnp.einsum("tkh,kch->tkc", up_back, up_w[0], preferred_element_type=jnp.float32)
    partial_sum = select_sum(back_gate, one_hot(gate_feat, feat_blocks, gate_live))
    partial_sum = partial_sum + select_sum(back_up, one_hot(up_feat, feat_blocks, up_live))
    pieces = partial_sum.astype(jnp.bfloat16).reshape(tokens_here, tensor_size, D // tensor_size)
    summed = add_sources(lax.all_to_all(pieces, "tensor", split_axis=1, concat_axis=1, tiled=True))
    grad_x = summed.astype(jnp.bfloat16)
    gate_sum, up_sum, down_sum = (
        lax.psum_scatter(
            gate_term.astype(jnp.bfloat16), "dp", scatter_dimension=2, tiled=True
        ).astype(jnp.float32),
        lax.psum_scatter(
            up_term.astype(jnp.bfloat16), "dp", scatter_dimension=2, tiled=True
        ).astype(jnp.float32),
        lax.psum_scatter(
            down_term.astype(jnp.bfloat16), "dp", scatter_dimension=2, tiled=True
        ).astype(jnp.float32),
    )
    return (
        grad_x,
        gate_sum.astype(jnp.bfloat16),
        up_sum.astype(jnp.bfloat16),
        down_sum.astype(jnp.bfloat16),
    )


def pair_tables(lists, hidden_rows, length):
    slots = lists.shape[1]
    live = lists >= 0
    clamped = jnp.maximum(lists, 0)
    feat, row = clamped // hidden_rows, clamped % hidden_rows
    hot = (row[:, :, None] == jnp.arange(hidden_rows)) & live[:, :, None]
    counts = jnp.sum(hot.astype(jnp.int32), axis=1)
    padded = (counts + 1) // 2 * 2
    order = jnp.arange(slots)
    same = (row[:, :, None] == row[:, None, :]) & (order[None, :] < order[:, None])
    rank = jnp.sum(same.astype(jnp.int32), axis=2)
    before = jnp.arange(hidden_rows) < row[:, :, None]
    start = jnp.sum(jnp.where(before, padded[:, None, :], 0), axis=2)
    place = jnp.where(live, start + rank, -1)
    here = place[:, :, None] == jnp.arange(length)
    slot = jnp.sum(jnp.where(here, (order - slots)[None, :, None], 0), axis=1) + slots
    feat_at = jnp.sum(jnp.where(here, feat[:, :, None], 0), axis=1)
    row_at = jnp.sum(jnp.where(here, row[:, :, None], 0), axis=1)
    pairs = jnp.sum(padded, axis=1) // 2
    living = jnp.sum(live.astype(jnp.int32), axis=1)
    return jnp.concatenate([slot, feat_at, row_at], axis=0), jnp.concatenate([pairs, living])


def nt_dot(a, b):
    return lax.dot_general(a, b, (((1,), (1,)), ((), ())), preferred_element_type=F32)


def layer_kernel(
    hidden_rows, feat_blocks, groups, tok, grad_scale,
    counts, tables, lists, both_hbm, gate_hbm, up_hbm, down_hbm,
    part_ref, ggw_ref, guw_ref, gdw_ref,
    xin, cot, gw, uw, dw, gate, up, gh, gg, gu, hid, xt, ht, dense, back_g, back_u, sems,
):
    slots = lists.shape[1]
    tokens = groups * tok
    rows = BLOCK // groups
    pick = groups
    me = lax.axis_index("dp")
    copies = [
        pltpu.make_async_copy(src, dst, sems.at[i])
        for i, (src, dst) in enumerate((
            (both_hbm.at[0], xin),
            (gate_hbm.at[0], gw.at[pl.ds(0, slots)]),
            (up_hbm.at[0], uw.at[pl.ds(0, slots)]),
            (both_hbm.at[1], cot),
            (down_hbm.at[0], dw.at[pl.ds(0, slots)]),
        ))
    ]
    for copy in copies:
        copy.start()
    blank = jnp.zeros((BLOCK, BLOCK), BF16)
    gw[slots] = blank
    uw[slots] = blank
    dw[slots] = blank

    @pl.loop(0, hidden_rows)
    def _(h):
        zero = jnp.zeros((tokens, BLOCK), F32)
        gate[h] = zero
        up[h] = zero
        gh[h] = zero

    @pl.loop(0, feat_blocks)
    def _(d):
        zero = jnp.zeros((tok, BLOCK), F32)
        back_g[d] = zero
        back_u[d] = zero

    for copy in copies:
        copy.wait()

    pairs = jnp.maximum(jnp.maximum(counts[0], counts[1]), counts[2])

    @pl.loop(0, (pairs + UNROLL - 1) // UNROLL)
    def _(t):
        for u in range(UNROLL):
            a = 2 * (t * UNROLL + u)
            b = a + 1
            for i, (acts, w, acc) in enumerate(((xin, gw, gate), (xin, uw, up), (cot, dw, gh))):
                left = jnp.concatenate([acts[tables[3 + i, a]], acts[tables[3 + i, b]]], axis=1)
                one, two = w[tables[i, a]], w[tables[i, b]]
                h = tables[6 + i, a]
                if i < 2:
                    got = jnp.dot(
                        left, jnp.concatenate([one, two], axis=0), preferred_element_type=F32
                    )
                else:
                    got = nt_dot(left, jnp.concatenate([one, two], axis=1))
                acc[h] += got

    @pl.loop(0, hidden_rows)
    def _(h):
        @pl.loop(0, tokens // 128)
        def _(r):
            at = pl.ds(pl.multiple_of(r * 128, 128), 128)
            g, u, y = gate[h, at], up[h, at], gh[h, at]
            sig = 1.0 / (1.0 + jnp.exp(-g))
            act = g * sig
            hid[h, at] = (act * u).astype(BF16)
            gg[h, at] = (y * u * sig * (1.0 + g * (1.0 - sig))).astype(BF16)
            gu[h, at] = (y * act).astype(BF16)

    own = pl.ds(pl.multiple_of(me * tok, tok), tok)
    living = jnp.maximum(counts[3], counts[4])

    @pl.loop(0, (living + BACK_UNROLL - 1) // BACK_UNROLL)
    def _(t):
        for u in range(BACK_UNROLL):
            k = t * BACK_UNROLL + u
            for i, (grad, w, acc) in enumerate(((gg, gw, back_g), (gu, uw, back_u))):
                e = lists[i, k]
                block = w[jnp.where(e >= 0, k, slots)]
                e = jnp.maximum(e, 0)
                acc[e // hidden_rows] += nt_dot(grad[e % hidden_rows, own], block)

    @pl.loop(0, feat_blocks)
    def _(d):
        part_ref[d] = (back_g[d] + back_u[d]).astype(BF16)

    line = lax.broadcasted_iota(jnp.int32, (pick * BLOCK, BLOCK), 0)
    lane = lax.broadcasted_iota(jnp.int32, (pick * BLOCK, BLOCK), 1)
    want = (lane // rows) * BLOCK + me * rows + lane % rows
    chooser = jnp.where(line == want, 1.0, 0.0).astype(BF16)

    def own_rows(src, dst, count):
        @pl.loop(0, count // pick)
        def _(g):
            wide = jnp.concatenate([src[g * pick + q] for q in range(pick)], axis=1)
            chosen = jnp.dot(wide, chooser, preferred_element_type=F32)
            at = pl.ds(pl.multiple_of(g * BLOCK, BLOCK), BLOCK)
            dst[at, :] = chosen.T.astype(BF16)

    own_rows(xin, xt, feat_blocks)
    own_rows(hid, ht, hidden_rows)

    def all_products(left, right, count):
        @pl.loop(0, count // 2)
        def _(n):
            two = jnp.concatenate([right[2 * n], right[2 * n + 1]], axis=1)
            got = jnp.dot(left[...], two, preferred_element_type=F32) * grad_scale
            got = got.astype(BF16)
            per = left.shape[0] // rows
            for s in range(2):
                dense[pl.ds((2 * n + s) * per, per)] = got[:, s * BLOCK:(s + 1) * BLOCK].reshape(
                    per, rows, BLOCK
                )

    def keep_live(i, out, by_feat):
        @pl.loop(0, slots // SLOT_UNROLL)
        def _(t):
            for u in range(SLOT_UNROLL):
                k = t * SLOT_UNROLL + u
                e = lists[i, k]
                c = jnp.maximum(e, 0)
                d, h = c // hidden_rows, c % hidden_rows
                at = d * hidden_rows + h if by_feat else h * feat_blocks + d
                block = dense[at]
                out[0, k] = jnp.where(e >= 0, block, jnp.zeros_like(block))

    all_products(xt, gg, hidden_rows)
    keep_live(0, ggw_ref, False)
    all_products(xt, gu, hidden_rows)
    keep_live(1, guw_ref, False)
    all_products(ht, cot, feat_blocks)
    keep_live(2, gdw_ref, True)


def layer(both, gate_w, up_w, down_w, lists, tables, counts, hidden_rows, groups):
    _, feat_blocks, tokens, _ = both.shape
    slots = lists.shape[1]
    tok = tokens // groups
    rows = BLOCK // groups
    grad_scale = 1.0 / math.sqrt(tokens)
    smem = pl.BlockSpec(memory_space=pltpu.SMEM)
    vmem = pl.BlockSpec(memory_space=pltpu.VMEM)
    hbm = pl.BlockSpec(memory_space=pl.ANY)
    weights = pltpu.VMEM((slots + 1, BLOCK, BLOCK), BF16)
    acts = pltpu.VMEM((feat_blocks, tokens, BLOCK), BF16)
    wide = pltpu.VMEM((hidden_rows, tokens, BLOCK), F32)
    narrow = pltpu.VMEM((hidden_rows, tokens, BLOCK), BF16)
    grad = jax.ShapeDtypeStruct((1, slots, rows, BLOCK), BF16)
    back = pltpu.VMEM((feat_blocks, tok, BLOCK), F32)
    return pl.pallas_call(
        functools.partial(layer_kernel, hidden_rows, feat_blocks, groups, tok, grad_scale),
        out_shape=(jax.ShapeDtypeStruct((feat_blocks, tok, BLOCK), BF16), grad, grad, grad),
        in_specs=[smem, smem, smem, hbm, hbm, hbm, hbm],
        out_specs=[vmem] * 4,
        scratch_shapes=[
            acts, acts, weights, weights, weights, wide, wide, wide, narrow, narrow, narrow,
            pltpu.VMEM((feat_blocks * rows, tokens), BF16),
            pltpu.VMEM((hidden_rows * rows, tokens), BF16),
            pltpu.VMEM((feat_blocks * hidden_rows, rows, BLOCK), BF16),
            back, back,
            pltpu.SemaphoreType.DMA((5,)),
        ],
        compiler_params=pltpu.CompilerParams(vmem_limit_bytes=60 * 1024 * 1024),
        name="layer",
    )(counts, tables, lists, both, gate_w, up_w, down_w)


def gather_kernel(
    span, x_ref, cot_ref, out, own, local, col_sent, cross_sent, side_sent, col_got, cross_got, side_got
):
    tok = x_ref.shape[0]
    mine = x_ref.shape[1] // BLOCK
    p, t = lax.axis_index("dp"), lax.axis_index("tensor")
    z, core = t // 2, t % 2
    over_x, over_y, corner = p + 1 - 2 * (p % 2), (p + 2) % 4, 3 - p
    other = t + 1 - 2 * core

    barrier = pltpu.get_barrier_semaphore()

    def greet(device):
        pl.semaphore_signal(barrier, inc=1, device_id=device, device_id_type=pl.DeviceIdType.MESH)

    greet((over_x, t))
    greet((over_y, t))
    greet((p, other))

    @pl.when(z > 0)
    def _():
        greet((p, t - 2))

    @pl.when(z < span - 1)
    def _():
        greet((p, t + 2))

    for b in range(mine):
        own[0, b] = x_ref[:, b * BLOCK:(b + 1) * BLOCK]
        own[1, b] = cot_ref[:, b * BLOCK:(b + 1) * BLOCK]

    inside = (z > 0) & (z < span - 1)

    @pl.when(inside)
    def _():
        pl.semaphore_wait(barrier, 5)

    @pl.when(jnp.logical_not(inside))
    def _():
        pl.semaphore_wait(barrier, 4)

    def region(group, level, which, array=None):
        blocks = pl.ds((level * 2 + which) * mine, mine)
        rows = pl.ds(pl.multiple_of(group * tok, tok), tok)
        if array is None:
            return out.at[:, blocks, rows]
        return out.at[array, blocks, rows]

    def copy(src, dst, sent, got, device):
        return pltpu.make_async_remote_copy(
            src_ref=src, dst_ref=dst, send_sem=sent, recv_sem=got,
            device_id=device, device_id_type=pl.DeviceIdType.MESH,
        )

    def along(level, way, src=None):
        here = region(p, level, core)
        return copy(
            here if src is None else src, here, col_sent.at[way, level], col_got.at[level],
            (p, t + 2 if way == 0 else t - 2),
        )

    def across(level, kind, src=None):
        if kind < 2:
            here = region(p, level, core)
        elif kind == 2:
            here = region(over_x, level, core, 0)
        else:
            here = region(over_y, level, core, 1)
        to = over_x if kind in (0, 3) else over_y
        return copy(
            here if src is None else src, here, cross_sent.at[kind, level], cross_got.at[kind, level],
            (to, t),
        )

    def aside(level, kind, src=None, which=core):
        here = (
            region(p, level, which), region(over_x, level, which), region(over_y, level, which),
            region(corner, level, which, 0), region(corner, level, which, 1),
        )[kind]
        return copy(
            here if src is None else src, here, side_sent.at[kind, level], side_got.at[kind, level],
            (p, other),
        )

    def column(level, sign):
        src = None
        if sign == 0:
            src = own
        else:
            along(level, 0).wait_recv()
        if sign <= 0:
            @pl.when(z < span - 1)
            def _():
                along(level, 0, src).start()
        if sign >= 0:
            @pl.when(z > 0)
            def _():
                along(level, 1, src).start()
        across(level, 0, src).start()
        across(level, 1, src).start()
        aside(level, 0, src).start()

    def cross(level, sign):
        copy(
            region(over_x, level, core), region(over_x, level, core), cross_sent.at[0, level],
            cross_got.at[0, level], (over_x, t),
        ).wait_recv()
        across(level, 2).start()
        aside(level, 1).start()
        copy(
            region(over_y, level, core), region(over_y, level, core), cross_sent.at[1, level],
            cross_got.at[1, level], (over_y, t),
        ).wait_recv()
        across(level, 3).start()
        aside(level, 2).start()

    def diagonal(level, sign):
        for kind in (2, 3):
            here = region(corner, level, core, kind - 2)
            copy(
                here, here, cross_sent.at[kind, level], cross_got.at[kind, level],
                (over_y if kind == 2 else over_x, t),
            ).wait_recv()
            aside(level, kind + 1).start()

    keep = pltpu.make_async_copy(own, region(p, z, core), local)
    keep.start()

    def at_distance(step, action):
        if step < 0 or step >= span:
            return
        if step == 0:
            action(z, 0)
            return

        @pl.when(z >= step)
        def _():
            action(z - step, -1)

        @pl.when(z + step < span)
        def _():
            action(z + step, 1)

    for step in range(span + 2):
        at_distance(step, column)
        at_distance(step - 1, cross)
        at_distance(step - 2, diagonal)

    keep.wait()
    for level in range(span):
        for kind in range(4):
            across(level, kind).wait_send()
        for kind in range(5):
            aside(level, kind).wait_send()
            aside(level, kind, which=1 - core).wait_recv()

        @pl.when((z >= level) & (z < span - 1))
        def _():
            along(level, 0).wait_send()

        @pl.when((z <= level) & (z > 0))
        def _():
            along(level, 1).wait_send()


def gather(inputs, cotangent, tensor_size, groups):
    tok, width = inputs.shape
    mine, span = width // BLOCK, tensor_size // 2
    vmem = pl.BlockSpec(memory_space=pltpu.VMEM)
    dma = pltpu.SemaphoreType.DMA
    return pl.pallas_call(
        functools.partial(gather_kernel, span),
        out_shape=jax.ShapeDtypeStruct((2, mine * tensor_size, tok * groups, BLOCK), BF16),
        in_specs=[vmem, vmem],
        out_specs=pl.BlockSpec(memory_space=pl.ANY),
        scratch_shapes=[
            pltpu.VMEM((2, mine, tok, BLOCK), BF16),
            dma(()),
            dma((2, span)), dma((4, span)), dma((5, span)),
            dma((span,)), dma((4, span)), dma((5, span)),
        ],
        compiler_params=pltpu.CompilerParams(
            collective_id=0, has_side_effects=True, vmem_limit_bytes=32 * 1024 * 1024
        ),
        name="gather",
    )(inputs, cotangent)


def on_device(inputs, cotangent, gate_w, up_w, down_w, gate_list, up_list, down_list):
    tensor_size, groups = lax.axis_size("tensor"), lax.axis_size("dp")
    hidden_rows = FF // (BLOCK * tensor_size)
    tok, width = inputs.shape
    mine = width // BLOCK
    slots = gate_list.shape[1]
    lists = jnp.concatenate([gate_list, up_list, down_list], axis=0)
    step = 2 * UNROLL
    length = (slots + hidden_rows + step - 1) // step * step
    tables, counts = pair_tables(lists, hidden_rows, length)

    both = gather(inputs, cotangent, tensor_size, groups)
    part, ggw, guw, gdw = layer(
        both, gate_w, up_w, down_w, lists, tables, counts, hidden_rows, groups
    )
    pieces = part.reshape(tensor_size, mine, tok, BLOCK)
    got = lax.all_to_all(pieces, "tensor", split_axis=0, concat_axis=0, tiled=True)
    summed = jnp.sum(got.astype(F32), axis=0).astype(BF16)
    grad_x = summed.transpose(1, 0, 2).reshape(tok, width)
    return grad_x, ggw, guw, gdw


def fits(mesh):
    return mesh.shape["dp"] == 4 and mesh.shape["tensor"] >= 4


def solution(mesh):
    return jax.shard_map(
        on_device if fits(mesh) else plain_on_device,
        mesh=mesh,
        in_specs=(
            P("dp", "tensor"),
            P("dp", "tensor"),
            P("tensor", None, None, None),
            P("tensor", None, None, None),
            P("tensor", None, None, None),
            P("tensor", None),
            P("tensor", None),
            P("tensor", None),
        ),
        out_specs=(
            P("dp", "tensor"),
            P("tensor", None, "dp", None),
            P("tensor", None, "dp", None),
            P("tensor", None, "dp", None),
        ),
        check_vma=False,
    )
```

```python
import functools
import math

import jax
import jax.numpy as jnp
from jax import lax
from jax.experimental import pallas as pl
from jax.experimental.pallas import tpu as pltpu
from jax.sharding import PartitionSpec as P

D = 4096
FF = 16384
BLOCK = 128
UNROLL = 4
BACK_UNROLL = 4
SLOT_UNROLL = 8
F32 = jnp.float32
BF16 = jnp.bfloat16


def decode(entries, row_count):
    living = entries >= 0
    clamped = jnp.maximum(entries, 0)
    return (living, clamped // row_count, clamped % row_count)


def one_hot(block_index, width_count, living):
    return ((block_index[:, None] == jnp.arange(width_count)[None, :]) & living[:, None]).astype(
        jnp.float32
    )


def select_sum(values, table):
    return jnp.sum(values[:, :, None, :] * table[None, :, :, None], axis=1)


def project_rows(blocks_in, weights, rows_hot):
    products = jnp.einsum("tkc,kch->tkh", blocks_in, weights, preferred_element_type=jnp.float32)
    return select_sum(products, rows_hot)


def weight_term(products, grad_scale, living):
    rounded = (products * grad_scale).astype(jnp.bfloat16)
    rounded = lax.optimization_barrier(rounded)
    return (rounded.astype(jnp.float32) * living[:, None, None].astype(jnp.float32))[None]


def add_sources(received):
    return jnp.sum(received.astype(jnp.float32), axis=1)


def plain_on_device(inputs, cotangent, gate_w, up_w, down_w, gate_list, up_list, down_list):
    tensor_size = lax.axis_size("tensor")
    hidden_rows = FF // (BLOCK * tensor_size)
    feat_blocks = D // BLOCK
    tokens_here = inputs.shape[0]
    grad_scale = 1.0 / math.sqrt(tokens_here * lax.axis_size("dp"))
    gate_live, gate_feat, gate_row = decode(gate_list[0], hidden_rows)
    up_live, up_feat, up_row = decode(up_list[0], hidden_rows)
    down_live, down_feat, down_row = decode(down_list[0], hidden_rows)
    whole_in, whole_cot = (
        lax.all_gather(inputs, "tensor", axis=1, tiled=True),
        lax.all_gather(cotangent, "tensor", axis=1, tiled=True),
    )
    input_blocks = whole_in.reshape(tokens_here, feat_blocks, BLOCK)
    gate_in = jnp.take(input_blocks, gate_feat, axis=1)
    up_in = jnp.take(input_blocks, up_feat, axis=1)
    gate_val = project_rows(gate_in, gate_w[0], one_hot(gate_row, hidden_rows, gate_live))
    up_val = project_rows(up_in, up_w[0], one_hot(up_row, hidden_rows, up_live))
    sigmoid_gate = jax.nn.sigmoid(gate_val)
    active = gate_val * sigmoid_gate
    hidden = (active * up_val).astype(jnp.bfloat16)
    cot_blocks = whole_cot.reshape(tokens_here, feat_blocks, BLOCK)
    down_cot = jnp.take(cot_blocks, down_feat, axis=1)
    hidden_down = jnp.take(hidden, down_row, axis=1)
    down_part = jnp.einsum("tkc,khc->tkh", down_cot, down_w[0], preferred_element_type=jnp.float32)
    grad_hidden = select_sum(down_part, one_hot(down_row, hidden_rows, down_live))
    down_term = weight_term(
        jnp.einsum("tkh,tkc->khc", hidden_down, down_cot, preferred_element_type=jnp.float32),
        grad_scale,
        down_live,
    )
    grad_gate = (
        grad_hidden * up_val * sigmoid_gate * (1.0 + gate_val * (1.0 - sigmoid_gate))
    ).astype(jnp.bfloat16)
    grad_up = (grad_hidden * active).astype(jnp.bfloat16)
    gate_back = jnp.take(grad_gate, gate_row, axis=1)
    up_back = jnp.take(grad_up, up_row, axis=1)
    gate_term = weight_term(
        jnp.einsum("tkc,tkh->kch", gate_in, gate_back, preferred_element_type=jnp.float32),
        grad_scale,
        gate_live,
    )
    up_term = weight_term(
        jnp.einsum("tkc,tkh->kch", up_in, up_back, preferred_element_type=jnp.float32),
        grad_scale,
        up_live,
    )
    back_gate = jnp.einsum("tkh,kch->tkc", gate_back, gate_w[0], preferred_element_type=jnp.float32)
    back_up = jnp.einsum("tkh,kch->tkc", up_back, up_w[0], preferred_element_type=jnp.float32)
    partial_sum = select_sum(back_gate, one_hot(gate_feat, feat_blocks, gate_live))
    partial_sum = partial_sum + select_sum(back_up, one_hot(up_feat, feat_blocks, up_live))
    pieces = partial_sum.astype(jnp.bfloat16).reshape(tokens_here, tensor_size, D // tensor_size)
    summed = add_sources(lax.all_to_all(pieces, "tensor", split_axis=1, concat_axis=1, tiled=True))
    grad_x = summed.astype(jnp.bfloat16)
    gate_sum, up_sum, down_sum = (
        lax.psum_scatter(
            gate_term.astype(jnp.bfloat16), "dp", scatter_dimension=2, tiled=True
        ).astype(jnp.float32),
        lax.psum_scatter(
            up_term.astype(jnp.bfloat16), "dp", scatter_dimension=2, tiled=True
        ).astype(jnp.float32),
        lax.psum_scatter(
            down_term.astype(jnp.bfloat16), "dp", scatter_dimension=2, tiled=True
        ).astype(jnp.float32),
    )
    return (
        grad_x,
        gate_sum.astype(jnp.bfloat16),
        up_sum.astype(jnp.bfloat16),
        down_sum.astype(jnp.bfloat16),
    )


def pair_tables(lists, hidden_rows, length):
    slots = lists.shape[1]
    live = lists >= 0
    clamped = jnp.maximum(lists, 0)
    feat, row = clamped // hidden_rows, clamped % hidden_rows
    hot = (row[:, :, None] == jnp.arange(hidden_rows)) & live[:, :, None]
    counts = jnp.sum(hot.astype(jnp.int32), axis=1)
    padded = (counts + 1) // 2 * 2
    order = jnp.arange(slots)
    same = (row[:, :, None] == row[:, None, :]) & (order[None, :] < order[:, None])
    rank = jnp.sum(same.astype(jnp.int32), axis=2)
    before = jnp.arange(hidden_rows) < row[:, :, None]
    start = jnp.sum(jnp.where(before, padded[:, None, :], 0), axis=2)
    place = jnp.where(live, start + rank, -1)
    here = place[:, :, None] == jnp.arange(length)
    slot = jnp.sum(jnp.where(here, (order - slots)[None, :, None], 0), axis=1) + slots
    feat_at = jnp.sum(jnp.where(here, feat[:, :, None], 0), axis=1)
    row_at = jnp.sum(jnp.where(here, row[:, :, None], 0), axis=1)
    pairs = jnp.sum(padded, axis=1) // 2
    living = jnp.sum(live.astype(jnp.int32), axis=1)
    return jnp.concatenate([slot, feat_at, row_at], axis=0), jnp.concatenate([pairs, living])


def nt_dot(a, b):
    return lax.dot_general(a, b, (((1,), (1,)), ((), ())), preferred_element_type=F32)


def layer_kernel(
    hidden_rows, feat_blocks, groups, tok, span,
    counts, tables, lists, both_hbm, gate_hbm, up_hbm, down_hbm,
    part_ref, gg_hbm, gu_hbm, xt_hbm, ht_hbm,
    xin, cot, gw, uw, dw, gate, up, gh, gg, gu, hid, xt, ht, back_g, back_u, sems, out_sems,
):
    slots = lists.shape[1]
    tokens = groups * tok
    rows = BLOCK // groups
    pick = groups
    mine = feat_blocks // (2 * span)
    me = lax.axis_index("dp")
    copies = [
        pltpu.make_async_copy(src, dst, sems.at[i])
        for i, (src, dst) in enumerate((
            (both_hbm.at[0], xin),
            (gate_hbm.at[0], gw.at[pl.ds(0, slots)]),
            (up_hbm.at[0], uw.at[pl.ds(0, slots)]),
            (both_hbm.at[1], cot),
            (down_hbm.at[0], dw.at[pl.ds(0, slots)]),
        ))
    ]
    for copy in copies:
        copy.start()
    blank = jnp.zeros((BLOCK, BLOCK), BF16)
    gw[slots] = blank
    uw[slots] = blank
    dw[slots] = blank

    @pl.loop(0, hidden_rows)
    def _(h):
        zero = jnp.zeros((tokens, BLOCK), F32)
        gate[h] = zero
        up[h] = zero
        gh[h] = zero

    @pl.loop(0, feat_blocks)
    def _(d):
        zero = jnp.zeros((tok, BLOCK), F32)
        back_g[d] = zero
        back_u[d] = zero

    def products(pairs, which):
        @pl.loop(0, (pairs + UNROLL - 1) // UNROLL)
        def _(t):
            for u in range(UNROLL):
                a = 2 * (t * UNROLL + u)
                b = a + 1
                for i, acts, w, acc in which:
                    left = jnp.concatenate([acts[tables[3 + i, a]], acts[tables[3 + i, b]]], axis=1)
                    one, two = w[tables[i, a]], w[tables[i, b]]
                    if i < 2:
                        found = jnp.dot(
                            left, jnp.concatenate([one, two], axis=0), preferred_element_type=F32
                        )
                    else:
                        found = nt_dot(left, jnp.concatenate([one, two], axis=1))
                    acc[tables[6 + i, a]] += found

    for copy in copies[:3]:
        copy.wait()
    products(jnp.maximum(counts[0], counts[1]), ((0, xin, gw, gate), (1, xin, uw, up)))
    for copy in copies[3:]:
        copy.wait()
    products(counts[2], ((2, cot, dw, gh),))

    @pl.loop(0, hidden_rows)
    def _(h):
        @pl.loop(0, tokens // 128)
        def _(r):
            at = pl.ds(pl.multiple_of(r * 128, 128), 128)
            g, u, y = gate[h, at], up[h, at], gh[h, at]
            sig = 1.0 / (1.0 + jnp.exp(-g))
            act = g * sig
            hid[h, at] = (act * u).astype(BF16)
            gg[h, at] = (y * u * sig * (1.0 + g * (1.0 - sig))).astype(BF16)
            gu[h, at] = (y * act).astype(BF16)

    leaving = [
        pltpu.make_async_copy(src, dst, out_sems.at[i])
        for i, (src, dst) in enumerate(((gg, gg_hbm), (gu, gu_hbm), (xt, xt_hbm), (ht, ht_hbm)))
    ]
    leaving[0].start()
    leaving[1].start()

    line = lax.broadcasted_iota(jnp.int32, (pick * BLOCK, BLOCK), 0)
    lane = lax.broadcasted_iota(jnp.int32, (pick * BLOCK, BLOCK), 1)
    want = (lane // rows) * BLOCK + me * rows + lane % rows
    chooser = jnp.where(line == want, 1.0, 0.0).astype(BF16)

    def own_rows(src, dst, count):
        @pl.loop(0, count // pick)
        def _(g):
            wide = jnp.concatenate([src[g * pick + q] for q in range(pick)], axis=1)
            chosen = jnp.dot(wide, chooser, preferred_element_type=F32)
            at = pl.ds(pl.multiple_of(g * BLOCK, BLOCK), BLOCK)
            dst[at, :] = chosen.T.astype(BF16)

    own_rows(xin, xt, feat_blocks)
    own_rows(hid, ht, hidden_rows)
    leaving[2].start()
    leaving[3].start()

    own = pl.ds(pl.multiple_of(me * tok, tok), tok)
    living = jnp.maximum(counts[3], counts[4])

    @pl.loop(0, (living + BACK_UNROLL - 1) // BACK_UNROLL)
    def _(t):
        for u in range(BACK_UNROLL):
            k = t * BACK_UNROLL + u
            for i, (grad, w, acc) in enumerate(((gg, gw, back_g), (gu, uw, back_u))):
                e = lists[i, k]
                block = w[jnp.where(e >= 0, k, slots)]
                e = jnp.maximum(e, 0)
                acc[e // hidden_rows] += nt_dot(grad[e % hidden_rows, own], block)

    @pl.loop(0, feat_blocks)
    def _(d):
        owner, b = d // mine, d % mine
        part_ref[owner % 2, owner // 2, b] = (back_g[d] + back_u[d]).astype(BF16)

    for copy in leaving:
        copy.wait()


def layer(both, gate_w, up_w, down_w, lists, tables, counts, hidden_rows, groups, span):
    _, feat_blocks, tokens, _ = both.shape
    slots = lists.shape[1]
    tok = tokens // groups
    rows = BLOCK // groups
    smem = pl.BlockSpec(memory_space=pltpu.SMEM)
    vmem = pl.BlockSpec(memory_space=pltpu.VMEM)
    hbm = pl.BlockSpec(memory_space=pl.ANY)
    weights = pltpu.VMEM((slots + 1, BLOCK, BLOCK), BF16)
    acts = pltpu.VMEM((feat_blocks, tokens, BLOCK), BF16)
    wide = pltpu.VMEM((hidden_rows, tokens, BLOCK), F32)
    narrow = pltpu.VMEM((hidden_rows, tokens, BLOCK), BF16)
    mine = feat_blocks // (2 * span)

    def leaves(*shape):
        return jax.ShapeDtypeStruct(shape, BF16)

    back = pltpu.VMEM((feat_blocks, tok, BLOCK), F32)
    return pl.pallas_call(
        functools.partial(layer_kernel, hidden_rows, feat_blocks, groups, tok, span),
        out_shape=(
            leaves(2, span, mine, tok, BLOCK),
            leaves(hidden_rows, tokens, BLOCK), leaves(hidden_rows, tokens, BLOCK),
            leaves(feat_blocks * rows, tokens), leaves(hidden_rows * rows, tokens),
        ),
        in_specs=[smem, smem, smem, hbm, hbm, hbm, hbm],
        out_specs=[vmem, hbm, hbm, hbm, hbm],
        scratch_shapes=[
            acts, acts, weights, weights, weights, wide, wide, wide, narrow, narrow, narrow,
            pltpu.VMEM((feat_blocks * rows, tokens), BF16),
            pltpu.VMEM((hidden_rows * rows, tokens), BF16),
            back, back,
            pltpu.SemaphoreType.DMA((5,)), pltpu.SemaphoreType.DMA((4,)),
        ],
        compiler_params=pltpu.CompilerParams(vmem_limit_bytes=60 * 1024 * 1024),
        name="layer",
    )(counts, tables, lists, both, gate_w, up_w, down_w)


def gather_kernel(
    span, x_ref, cot_ref, out, own, local, col_sent, cross_sent, side_sent, col_got, cross_got, side_got
):
    tok = x_ref.shape[0]
    mine = x_ref.shape[1] // BLOCK
    p, t = lax.axis_index("dp"), lax.axis_index("tensor")
    z, core = t // 2, t % 2
    over_x, over_y, corner = p + 1 - 2 * (p % 2), (p + 2) % 4, 3 - p
    other = t + 1 - 2 * core

    barrier = pltpu.get_barrier_semaphore()

    def greet(device):
        pl.semaphore_signal(barrier, inc=1, device_id=device, device_id_type=pl.DeviceIdType.MESH)

    greet((over_x, t))
    greet((over_y, t))
    greet((p, other))

    @pl.when(z > 0)
    def _():
        greet((p, t - 2))

    @pl.when(z < span - 1)
    def _():
        greet((p, t + 2))

    for b in range(mine):
        own[0, b] = x_ref[:, b * BLOCK:(b + 1) * BLOCK]
        own[1, b] = cot_ref[:, b * BLOCK:(b + 1) * BLOCK]

    inside = (z > 0) & (z < span - 1)

    @pl.when(inside)
    def _():
        pl.semaphore_wait(barrier, 5)

    @pl.when(jnp.logical_not(inside))
    def _():
        pl.semaphore_wait(barrier, 4)

    def region(group, level, which, array=None):
        blocks = pl.ds((level * 2 + which) * mine, mine)
        rows = pl.ds(pl.multiple_of(group * tok, tok), tok)
        if array is None:
            return out.at[:, blocks, rows]
        return out.at[array, blocks, rows]

    def copy(src, dst, sent, got, device):
        return pltpu.make_async_remote_copy(
            src_ref=src, dst_ref=dst, send_sem=sent, recv_sem=got,
            device_id=device, device_id_type=pl.DeviceIdType.MESH,
        )

    def along(level, way, src=None):
        here = region(p, level, core)
        return copy(
            here if src is None else src, here, col_sent.at[way, level], col_got.at[level],
            (p, t + 2 if way == 0 else t - 2),
        )

    def across(level, kind, src=None):
        if kind < 2:
            here = region(p, level, core)
        elif kind == 2:
            here = region(over_x, level, core, 0)
        else:
            here = region(over_y, level, core, 1)
        to = over_x if kind in (0, 3) else over_y
        return copy(
            here if src is None else src, here, cross_sent.at[kind, level], cross_got.at[kind, level],
            (to, t),
        )

    def aside(level, kind, src=None, which=core):
        here = (
            region(p, level, which), region(over_x, level, which), region(over_y, level, which),
            region(corner, level, which, 0), region(corner, level, which, 1),
        )[kind]
        return copy(
            here if src is None else src, here, side_sent.at[kind, level], side_got.at[kind, level],
            (p, other),
        )

    def column(level, sign):
        src = None
        if sign == 0:
            src = own
        else:
            along(level, 0).wait_recv()
        if sign <= 0:
            @pl.when(z < span - 1)
            def _():
                along(level, 0, src).start()
        if sign >= 0:
            @pl.when(z > 0)
            def _():
                along(level, 1, src).start()
        across(level, 0, src).start()
        across(level, 1, src).start()
        aside(level, 0, src).start()

    def cross(level, sign):
        copy(
            region(over_x, level, core), region(over_x, level, core), cross_sent.at[0, level],
            cross_got.at[0, level], (over_x, t),
        ).wait_recv()
        across(level, 2).start()
        aside(level, 1).start()
        copy(
            region(over_y, level, core), region(over_y, level, core), cross_sent.at[1, level],
            cross_got.at[1, level], (over_y, t),
        ).wait_recv()
        across(level, 3).start()
        aside(level, 2).start()

    def diagonal(level, sign):
        for kind in (2, 3):
            here = region(corner, level, core, kind - 2)
            copy(
                here, here, cross_sent.at[kind, level], cross_got.at[kind, level],
                (over_y if kind == 2 else over_x, t),
            ).wait_recv()
            aside(level, kind + 1).start()

    keep = pltpu.make_async_copy(own, region(p, z, core), local)
    keep.start()

    def at_distance(step, action):
        if step < 0 or step >= span:
            return
        if step == 0:
            action(z, 0)
            return

        @pl.when(z >= step)
        def _():
            action(z - step, -1)

        @pl.when(z + step < span)
        def _():
            action(z + step, 1)

    for step in range(span + 2):
        at_distance(step, column)
        at_distance(step - 1, cross)
        at_distance(step - 2, diagonal)

    keep.wait()
    for level in range(span):
        for kind in range(4):
            across(level, kind).wait_send()
        for kind in range(5):
            aside(level, kind).wait_send()
            aside(level, kind, which=1 - core).wait_recv()

        @pl.when((z >= level) & (z < span - 1))
        def _():
            along(level, 0).wait_send()

        @pl.when((z <= level) & (z > 0))
        def _():
            along(level, 1).wait_send()


def gather(inputs, cotangent, tensor_size, groups):
    tok, width = inputs.shape
    mine, span = width // BLOCK, tensor_size // 2
    vmem = pl.BlockSpec(memory_space=pltpu.VMEM)
    dma = pltpu.SemaphoreType.DMA
    return pl.pallas_call(
        functools.partial(gather_kernel, span),
        out_shape=jax.ShapeDtypeStruct((2, mine * tensor_size, tok * groups, BLOCK), BF16),
        in_specs=[vmem, vmem],
        out_specs=pl.BlockSpec(memory_space=pl.ANY),
        scratch_shapes=[
            pltpu.VMEM((2, mine, tok, BLOCK), BF16),
            dma(()),
            dma((2, span)), dma((4, span)), dma((5, span)),
            dma((span,)), dma((4, span)), dma((5, span)),
        ],
        compiler_params=pltpu.CompilerParams(
            collective_id=0, has_side_effects=True, vmem_limit_bytes=60 * 1024 * 1024
        ),
        name="gather",
    )(inputs, cotangent)


def finish_kernel(
    hidden_rows, feat_blocks, groups, span, grad_scale,
    lists, part, gg_hbm, gu_hbm, xt_hbm, ht_hbm, both_hbm,
    gx_ref, ggw_ref, guw_ref, gdw_ref,
    gg, gu, xt, ht, cot, dense, pair_in, pair_sum, peer_in, loads, pair_sems, sent, got,
):
    slots = lists.shape[1]
    rows = BLOCK // groups
    mine = feat_blocks // (2 * span)
    p, t = lax.axis_index("dp"), lax.axis_index("tensor")
    z, core = t // 2, t % 2
    other = t + 1 - 2 * core
    load_gg, load_xt, load_gu, load_ht, load_cot = [
        pltpu.make_async_copy(src, dst, loads.at[i])
        for i, (src, dst) in enumerate((
            (gg_hbm, gg), (xt_hbm, xt), (gu_hbm, gu), (ht_hbm, ht), (both_hbm.at[1], cot),
        ))
    ]

    barrier = pltpu.get_barrier_semaphore()

    def greet(device):
        pl.semaphore_signal(barrier, inc=1, device_id=device, device_id_type=pl.DeviceIdType.MESH)

    greet((p, other))
    for step in range(1, span):
        greet((p, (t + 2 * step) % (2 * span)))
    for load in (load_gg, load_xt, load_gu, load_ht, load_cot):
        load.start()
    pl.semaphore_wait(barrier, span)

    pair = pltpu.make_async_remote_copy(
        src_ref=part.at[1 - core], dst_ref=pair_in, send_sem=pair_sems.at[0], recv_sem=pair_sems.at[1],
        device_id=(p, other), device_id_type=pl.DeviceIdType.MESH,
    )
    pair.start()
    pair.wait_recv()

    def to_peer(step):
        to = (z + step) % span
        return pltpu.make_async_remote_copy(
            src_ref=pair_sum.at[to], dst_ref=peer_in.at[z], send_sem=sent.at[step],
            recv_sem=got.at[z], device_id=(p, to * 2 + core), device_id_type=pl.DeviceIdType.MESH,
        )

    for step in [*range(1, span), 0]:
        to = (z + step) % span

        @pl.loop(0, mine)
        def _(b):
            pair_sum[to, b] = (part[core, to, b].astype(F32) + pair_in[to, b].astype(F32)).astype(BF16)

        if step:
            to_peer(step).start()

    def all_products(left, right, count):
        @pl.loop(0, count // 2)
        def _(n):
            two = jnp.concatenate([right[2 * n], right[2 * n + 1]], axis=1)
            found = jnp.dot(left[...], two, preferred_element_type=F32) * grad_scale
            found = found.astype(BF16)
            per = left.shape[0] // rows
            for s in range(2):
                dense[pl.ds((2 * n + s) * per, per)] = found[:, s * BLOCK:(s + 1) * BLOCK].reshape(
                    per, rows, BLOCK
                )

    def keep_live(i, out, by_feat):
        @pl.loop(0, slots // SLOT_UNROLL)
        def _(n):
            for u in range(SLOT_UNROLL):
                k = n * SLOT_UNROLL + u
                e = lists[i, k]
                c = jnp.maximum(e, 0)
                d, h = c // hidden_rows, c % hidden_rows
                at = d * hidden_rows + h if by_feat else h * feat_blocks + d
                block = dense[at]
                out[0, k] = jnp.where(e >= 0, block, jnp.zeros_like(block))

    load_gg.wait()
    load_xt.wait()
    all_products(xt, gg, hidden_rows)
    keep_live(0, ggw_ref, False)
    load_gu.wait()
    all_products(xt, gu, hidden_rows)
    keep_live(1, guw_ref, False)
    load_ht.wait()
    load_cot.wait()
    all_products(ht, cot, feat_blocks)
    keep_live(2, gdw_ref, True)

    for step in range(1, span):
        at = (z + step) % span
        pltpu.make_async_remote_copy(
            src_ref=pair_sum.at[at], dst_ref=peer_in.at[at], send_sem=sent.at[step],
            recv_sem=got.at[at], device_id=(p, at * 2 + core), device_id_type=pl.DeviceIdType.MESH,
        ).wait_recv()
    for b in range(mine):
        total = pair_sum[z, b].astype(F32)
        for step in range(1, span):
            total = total + peer_in[(z + step) % span, b].astype(F32)
        gx_ref[:, b * BLOCK:(b + 1) * BLOCK] = total.astype(BF16)
    pair.wait_send()
    for step in range(1, span):
        to_peer(step).wait_send()


def finish(part, gg, gu, xt, ht, both, lists, tensor_size, groups):
    hidden_rows, tokens, _ = gg.shape
    feat_blocks = both.shape[1]
    slots = lists.shape[1]
    tok, rows, span = tokens // groups, BLOCK // groups, tensor_size // 2
    mine = feat_blocks // tensor_size
    smem = pl.BlockSpec(memory_space=pltpu.SMEM)
    vmem = pl.BlockSpec(memory_space=pltpu.VMEM)
    hbm = pl.BlockSpec(memory_space=pl.ANY)
    dma = pltpu.SemaphoreType.DMA
    grad = jax.ShapeDtypeStruct((1, slots, rows, BLOCK), BF16)
    bound = pltpu.VMEM((span, mine, tok, BLOCK), BF16)
    return pl.pallas_call(
        functools.partial(
            finish_kernel, hidden_rows, feat_blocks, groups, span, 1.0 / math.sqrt(tokens)
        ),
        out_shape=(jax.ShapeDtypeStruct((tok, mine * BLOCK), BF16), grad, grad, grad),
        in_specs=[smem, vmem, hbm, hbm, hbm, hbm, hbm],
        out_specs=[vmem] * 4,
        scratch_shapes=[
            pltpu.VMEM(gg.shape, BF16), pltpu.VMEM(gu.shape, BF16),
            pltpu.VMEM(xt.shape, BF16), pltpu.VMEM(ht.shape, BF16),
            pltpu.VMEM((feat_blocks, tokens, BLOCK), BF16),
            pltpu.VMEM((feat_blocks * hidden_rows, rows, BLOCK), BF16),
            bound, bound, bound,
            dma((5,)), dma((2,)), dma((span,)), dma((span,)),
        ],
        compiler_params=pltpu.CompilerParams(
            collective_id=1, has_side_effects=True, vmem_limit_bytes=60 * 1024 * 1024
        ),
        name="finish",
    )(lists, part, gg, gu, xt, ht, both)


def on_device(inputs, cotangent, gate_w, up_w, down_w, gate_list, up_list, down_list):
    tensor_size, groups = lax.axis_size("tensor"), lax.axis_size("dp")
    hidden_rows = FF // (BLOCK * tensor_size)
    slots = gate_list.shape[1]
    lists = jnp.concatenate([gate_list, up_list, down_list], axis=0)
    step = 2 * UNROLL
    length = (slots + hidden_rows + step - 1) // step * step
    tables, counts = pair_tables(lists, hidden_rows, length)

    both = gather(inputs, cotangent, tensor_size, groups)
    part, gg, gu, xt, ht = layer(
        both, gate_w, up_w, down_w, lists, tables, counts, hidden_rows, groups, tensor_size // 2
    )
    return finish(part, gg, gu, xt, ht, both, lists, tensor_size, groups)


def fits(mesh):
    return mesh.shape["dp"] == 4 and mesh.shape["tensor"] >= 4


def solution(mesh):
    return jax.shard_map(
        on_device if fits(mesh) else plain_on_device,
        mesh=mesh,
        in_specs=(
            P("dp", "tensor"),
            P("dp", "tensor"),
            P("tensor", None, None, None),
            P("tensor", None, None, None),
            P("tensor", None, None, None),
            P("tensor", None),
            P("tensor", None),
            P("tensor", None),
        ),
        out_specs=(
            P("dp", "tensor"),
            P("tensor", None, "dp", None),
            P("tensor", None, "dp", None),
            P("tensor", None, "dp", None),
        ),
        check_vma=False,
    )
```

```python
import functools
import math

import jax
import jax.numpy as jnp
from jax import lax
from jax.experimental import pallas as pl
from jax.experimental.pallas import tpu as pltpu
from jax.sharding import PartitionSpec as P

D = 4096
FF = 16384
BLOCK = 128
UNROLL = 4
BACK_UNROLL = 4
SLOT_UNROLL = 8
F32 = jnp.float32
BF16 = jnp.bfloat16


def decode(entries, row_count):
    living = entries >= 0
    clamped = jnp.maximum(entries, 0)
    return (living, clamped // row_count, clamped % row_count)


def one_hot(block_index, width_count, living):
    return ((block_index[:, None] == jnp.arange(width_count)[None, :]) & living[:, None]).astype(
        jnp.float32
    )


def select_sum(values, table):
    return jnp.sum(values[:, :, None, :] * table[None, :, :, None], axis=1)


def project_rows(blocks_in, weights, rows_hot):
    products = jnp.einsum("tkc,kch->tkh", blocks_in, weights, preferred_element_type=jnp.float32)
    return select_sum(products, rows_hot)


def weight_term(products, grad_scale, living):
    rounded = (products * grad_scale).astype(jnp.bfloat16)
    rounded = lax.optimization_barrier(rounded)
    return (rounded.astype(jnp.float32) * living[:, None, None].astype(jnp.float32))[None]


def add_sources(received):
    return jnp.sum(received.astype(jnp.float32), axis=1)


def plain_on_device(inputs, cotangent, gate_w, up_w, down_w, gate_list, up_list, down_list):
    tensor_size = lax.axis_size("tensor")
    hidden_rows = FF // (BLOCK * tensor_size)
    feat_blocks = D // BLOCK
    tokens_here = inputs.shape[0]
    grad_scale = 1.0 / math.sqrt(tokens_here * lax.axis_size("dp"))
    gate_live, gate_feat, gate_row = decode(gate_list[0], hidden_rows)
    up_live, up_feat, up_row = decode(up_list[0], hidden_rows)
    down_live, down_feat, down_row = decode(down_list[0], hidden_rows)
    whole_in, whole_cot = (
        lax.all_gather(inputs, "tensor", axis=1, tiled=True),
        lax.all_gather(cotangent, "tensor", axis=1, tiled=True),
    )
    input_blocks = whole_in.reshape(tokens_here, feat_blocks, BLOCK)
    gate_in = jnp.take(input_blocks, gate_feat, axis=1)
    up_in = jnp.take(input_blocks, up_feat, axis=1)
    gate_val = project_rows(gate_in, gate_w[0], one_hot(gate_row, hidden_rows, gate_live))
    up_val = project_rows(up_in, up_w[0], one_hot(up_row, hidden_rows, up_live))
    sigmoid_gate = jax.nn.sigmoid(gate_val)
    active = gate_val * sigmoid_gate
    hidden = (active * up_val).astype(jnp.bfloat16)
    cot_blocks = whole_cot.reshape(tokens_here, feat_blocks, BLOCK)
    down_cot = jnp.take(cot_blocks, down_feat, axis=1)
    hidden_down = jnp.take(hidden, down_row, axis=1)
    down_part = jnp.einsum("tkc,khc->tkh", down_cot, down_w[0], preferred_element_type=jnp.float32)
    grad_hidden = select_sum(down_part, one_hot(down_row, hidden_rows, down_live))
    down_term = weight_term(
        jnp.einsum("tkh,tkc->khc", hidden_down, down_cot, preferred_element_type=jnp.float32),
        grad_scale,
        down_live,
    )
    grad_gate = (
        grad_hidden * up_val * sigmoid_gate * (1.0 + gate_val * (1.0 - sigmoid_gate))
    ).astype(jnp.bfloat16)
    grad_up = (grad_hidden * active).astype(jnp.bfloat16)
    gate_back = jnp.take(grad_gate, gate_row, axis=1)
    up_back = jnp.take(grad_up, up_row, axis=1)
    gate_term = weight_term(
        jnp.einsum("tkc,tkh->kch", gate_in, gate_back, preferred_element_type=jnp.float32),
        grad_scale,
        gate_live,
    )
    up_term = weight_term(
        jnp.einsum("tkc,tkh->kch", up_in, up_back, preferred_element_type=jnp.float32),
        grad_scale,
        up_live,
    )
    back_gate = jnp.einsum("tkh,kch->tkc", gate_back, gate_w[0], preferred_element_type=jnp.float32)
    back_up = jnp.einsum("tkh,kch->tkc", up_back, up_w[0], preferred_element_type=jnp.float32)
    partial_sum = select_sum(back_gate, one_hot(gate_feat, feat_blocks, gate_live))
    partial_sum = partial_sum + select_sum(back_up, one_hot(up_feat, feat_blocks, up_live))
    pieces = partial_sum.astype(jnp.bfloat16).reshape(tokens_here, tensor_size, D // tensor_size)
    summed = add_sources(lax.all_to_all(pieces, "tensor", split_axis=1, concat_axis=1, tiled=True))
    grad_x = summed.astype(jnp.bfloat16)
    gate_sum, up_sum, down_sum = (
        lax.psum_scatter(
            gate_term.astype(jnp.bfloat16), "dp", scatter_dimension=2, tiled=True
        ).astype(jnp.float32),
        lax.psum_scatter(
            up_term.astype(jnp.bfloat16), "dp", scatter_dimension=2, tiled=True
        ).astype(jnp.float32),
        lax.psum_scatter(
            down_term.astype(jnp.bfloat16), "dp", scatter_dimension=2, tiled=True
        ).astype(jnp.float32),
    )
    return (
        grad_x,
        gate_sum.astype(jnp.bfloat16),
        up_sum.astype(jnp.bfloat16),
        down_sum.astype(jnp.bfloat16),
    )


def pair_tables(lists, hidden_rows, length):
    slots = lists.shape[1]
    live = lists >= 0
    clamped = jnp.maximum(lists, 0)
    feat, row = clamped // hidden_rows, clamped % hidden_rows
    hot = (row[:, :, None] == jnp.arange(hidden_rows)) & live[:, :, None]
    counts = jnp.sum(hot.astype(jnp.int32), axis=1)
    padded = (counts + 1) // 2 * 2
    order = jnp.arange(slots)
    same = (row[:, :, None] == row[:, None, :]) & (order[None, :] < order[:, None])
    rank = jnp.sum(same.astype(jnp.int32), axis=2)
    before = jnp.arange(hidden_rows) < row[:, :, None]
    start = jnp.sum(jnp.where(before, padded[:, None, :], 0), axis=2)
    place = jnp.where(live, start + rank, -1)
    here = place[:, :, None] == jnp.arange(length)
    slot = jnp.sum(jnp.where(here, (order - slots)[None, :, None], 0), axis=1) + slots
    feat_at = jnp.sum(jnp.where(here, feat[:, :, None], 0), axis=1)
    row_at = jnp.sum(jnp.where(here, row[:, :, None], 0), axis=1)
    pairs = jnp.sum(padded, axis=1) // 2
    living = jnp.sum(live.astype(jnp.int32), axis=1)
    return jnp.concatenate([slot, feat_at, row_at], axis=0), jnp.concatenate([pairs, living])


def nt_dot(a, b):
    return lax.dot_general(a, b, (((1,), (1,)), ((), ())), preferred_element_type=F32)


def layer_kernel(
    hidden_rows, feat_blocks, groups, tok, span,
    counts, tables, lists, both_hbm, gate_hbm, up_hbm, down_hbm,
    part_ref, gg_hbm, gu_hbm, xt_hbm, ht_hbm,
    xin, cot, gw, uw, dw, gate, up, gh, gg, gu, hid, xt, ht, back_g, back_u, sems, out_sems,
):
    slots = lists.shape[1]
    tokens = groups * tok
    rows = BLOCK // groups
    pick = groups
    mine = feat_blocks // (2 * span)
    me = lax.axis_index("dp")
    copies = [
        pltpu.make_async_copy(src, dst, sems.at[i])
        for i, (src, dst) in enumerate((
            (both_hbm.at[0], xin),
            (gate_hbm.at[0], gw.at[pl.ds(0, slots)]),
            (up_hbm.at[0], uw.at[pl.ds(0, slots)]),
            (both_hbm.at[1], cot),
            (down_hbm.at[0], dw.at[pl.ds(0, slots)]),
        ))
    ]
    for copy in copies:
        copy.start()
    blank = jnp.zeros((BLOCK, BLOCK), BF16)
    gw[slots] = blank
    uw[slots] = blank
    dw[slots] = blank

    @pl.loop(0, hidden_rows)
    def _(h):
        zero = jnp.zeros((tokens, BLOCK), F32)
        gate[h] = zero
        up[h] = zero
        gh[h] = zero

    @pl.loop(0, feat_blocks)
    def _(d):
        zero = jnp.zeros((tok, BLOCK), F32)
        back_g[d] = zero
        back_u[d] = zero

    def products(pairs, which):
        @pl.loop(0, (pairs + UNROLL - 1) // UNROLL)
        def _(t):
            for u in range(UNROLL):
                a = 2 * (t * UNROLL + u)
                b = a + 1
                for i, acts, w, acc in which:
                    left = jnp.concatenate([acts[tables[3 + i, a]], acts[tables[3 + i, b]]], axis=1)
                    one, two = w[tables[i, a]], w[tables[i, b]]
                    if i < 2:
                        found = jnp.dot(
                            left, jnp.concatenate([one, two], axis=0), preferred_element_type=F32
                        )
                    else:
                        found = nt_dot(left, jnp.concatenate([one, two], axis=1))
                    acc[tables[6 + i, a]] += found

    for copy in copies[:3]:
        copy.wait()
    products(jnp.maximum(counts[0], counts[1]), ((0, xin, gw, gate), (1, xin, uw, up)))
    for copy in copies[3:]:
        copy.wait()
    products(counts[2], ((2, cot, dw, gh),))

    @pl.loop(0, hidden_rows)
    def _(h):
        @pl.loop(0, tokens // 128)
        def _(r):
            at = pl.ds(pl.multiple_of(r * 128, 128), 128)
            g, u, y = gate[h, at], up[h, at], gh[h, at]
            sig = 1.0 / (1.0 + jnp.exp(-g))
            act = g * sig
            hid[h, at] = (act * u).astype(BF16)
            gg[h, at] = (y * u * sig * (1.0 + g * (1.0 - sig))).astype(BF16)
            gu[h, at] = (y * act).astype(BF16)

    leaving = [
        pltpu.make_async_copy(src, dst, out_sems.at[i])
        for i, (src, dst) in enumerate(((gg, gg_hbm), (gu, gu_hbm), (xt, xt_hbm), (ht, ht_hbm)))
    ]
    leaving[0].start()
    leaving[1].start()

    line = lax.broadcasted_iota(jnp.int32, (pick * BLOCK, BLOCK), 0)
    lane = lax.broadcasted_iota(jnp.int32, (pick * BLOCK, BLOCK), 1)
    want = (lane // rows) * BLOCK + me * rows + lane % rows
    chooser = jnp.where(line == want, 1.0, 0.0).astype(BF16)

    def own_rows(src, dst, count):
        @pl.loop(0, count // pick)
        def _(g):
            wide = jnp.concatenate([src[g * pick + q] for q in range(pick)], axis=1)
            chosen = jnp.dot(wide, chooser, preferred_element_type=F32)
            at = pl.ds(pl.multiple_of(g * BLOCK, BLOCK), BLOCK)
            dst[at, :] = chosen.T.astype(BF16)

    own_rows(xin, xt, feat_blocks)
    own_rows(hid, ht, hidden_rows)
    leaving[2].start()
    leaving[3].start()

    own = pl.ds(pl.multiple_of(me * tok, tok), tok)
    living = jnp.maximum(counts[3], counts[4])

    @pl.loop(0, (living + BACK_UNROLL - 1) // BACK_UNROLL)
    def _(t):
        for u in range(BACK_UNROLL):
            k = t * BACK_UNROLL + u
            for i, (grad, w, acc) in enumerate(((gg, gw, back_g), (gu, uw, back_u))):
                e = lists[i, k]
                block = w[jnp.where(e >= 0, k, slots)]
                e = jnp.maximum(e, 0)
                acc[e // hidden_rows] += nt_dot(grad[e % hidden_rows, own], block)

    @pl.loop(0, feat_blocks)
    def _(d):
        owner, b = d // mine, d % mine
        part_ref[owner % 2, owner // 2, b] = (back_g[d] + back_u[d]).astype(BF16)

    for copy in leaving:
        copy.wait()


def layer(both, gate_w, up_w, down_w, lists, tables, counts, hidden_rows, groups, span):
    _, feat_blocks, tokens, _ = both.shape
    slots = lists.shape[1]
    tok = tokens // groups
    rows = BLOCK // groups
    smem = pl.BlockSpec(memory_space=pltpu.SMEM)
    vmem = pl.BlockSpec(memory_space=pltpu.VMEM)
    hbm = pl.BlockSpec(memory_space=pl.ANY)
    weights = pltpu.VMEM((slots + 1, BLOCK, BLOCK), BF16)
    acts = pltpu.VMEM((feat_blocks, tokens, BLOCK), BF16)
    wide = pltpu.VMEM((hidden_rows, tokens, BLOCK), F32)
    narrow = pltpu.VMEM((hidden_rows, tokens, BLOCK), BF16)
    mine = feat_blocks // (2 * span)

    def leaves(*shape):
        return jax.ShapeDtypeStruct(shape, BF16)

    back = pltpu.VMEM((feat_blocks, tok, BLOCK), F32)
    return pl.pallas_call(
        functools.partial(layer_kernel, hidden_rows, feat_blocks, groups, tok, span),
        out_shape=(
            leaves(2, span, mine, tok, BLOCK),
            leaves(hidden_rows, tokens, BLOCK), leaves(hidden_rows, tokens, BLOCK),
            leaves(feat_blocks * rows, tokens), leaves(hidden_rows * rows, tokens),
        ),
        in_specs=[smem, smem, smem, hbm, hbm, hbm, hbm],
        out_specs=[vmem, hbm, hbm, hbm, hbm],
        scratch_shapes=[
            acts, acts, weights, weights, weights, wide, wide, wide, narrow, narrow, narrow,
            pltpu.VMEM((feat_blocks * rows, tokens), BF16),
            pltpu.VMEM((hidden_rows * rows, tokens), BF16),
            back, back,
            pltpu.SemaphoreType.DMA((5,)), pltpu.SemaphoreType.DMA((4,)),
        ],
        compiler_params=pltpu.CompilerParams(vmem_limit_bytes=60 * 1024 * 1024),
        name="layer",
    )(counts, tables, lists, both, gate_w, up_w, down_w)


def gather_kernel(
    span, x_ref, cot_ref, out, own, local, col_sent, cross_sent, side_sent, col_got, cross_got, side_got
):
    tok = x_ref.shape[0]
    mine = x_ref.shape[1] // BLOCK
    p, t = lax.axis_index("dp"), lax.axis_index("tensor")
    z, core = t // 2, t % 2
    over_x, over_y, corner = p + 1 - 2 * (p % 2), (p + 2) % 4, 3 - p
    other = t + 1 - 2 * core

    barrier = pltpu.get_barrier_semaphore()

    def greet(device):
        pl.semaphore_signal(barrier, inc=1, device_id=device, device_id_type=pl.DeviceIdType.MESH)

    greet((over_x, t))
    greet((over_y, t))
    greet((p, other))

    @pl.when(z > 0)
    def _():
        greet((p, t - 2))

    @pl.when(z < span - 1)
    def _():
        greet((p, t + 2))

    for b in range(mine):
        own[0, b] = x_ref[:, b * BLOCK:(b + 1) * BLOCK]
        own[1, b] = cot_ref[:, b * BLOCK:(b + 1) * BLOCK]

    inside = (z > 0) & (z < span - 1)

    @pl.when(inside)
    def _():
        pl.semaphore_wait(barrier, 5)

    @pl.when(jnp.logical_not(inside))
    def _():
        pl.semaphore_wait(barrier, 4)

    def region(group, level, which, array=None):
        blocks = pl.ds((level * 2 + which) * mine, mine)
        rows = pl.ds(pl.multiple_of(group * tok, tok), tok)
        if array is None:
            return out.at[:, blocks, rows]
        return out.at[array, blocks, rows]

    def copy(src, dst, sent, got, device):
        return pltpu.make_async_remote_copy(
            src_ref=src, dst_ref=dst, send_sem=sent, recv_sem=got,
            device_id=device, device_id_type=pl.DeviceIdType.MESH,
        )

    def along(level, way, src=None):
        here = region(p, level, core)
        return copy(
            here if src is None else src, here, col_sent.at[way, level], col_got.at[level],
            (p, t + 2 if way == 0 else t - 2),
        )

    def across(level, kind, src=None):
        if kind < 2:
            here = region(p, level, core)
        elif kind == 2:
            here = region(over_x, level, core, 0)
        else:
            here = region(over_y, level, core, 1)
        to = over_x if kind in (0, 3) else over_y
        return copy(
            here if src is None else src, here, cross_sent.at[kind, level], cross_got.at[kind, level],
            (to, t),
        )

    def aside(level, kind, src=None, which=core):
        here = (
            region(p, level, which), region(over_x, level, which), region(over_y, level, which),
            region(corner, level, which, 0), region(corner, level, which, 1),
        )[kind]
        return copy(
            here if src is None else src, here, side_sent.at[kind, level], side_got.at[kind, level],
            (p, other),
        )

    def column(level, sign):
        src = None
        if sign == 0:
            src = own
        else:
            along(level, 0).wait_recv()
        if sign <= 0:
            @pl.when(z < span - 1)
            def _():
                along(level, 0, src).start()
        if sign >= 0:
            @pl.when(z > 0)
            def _():
                along(level, 1, src).start()
        across(level, 0, src).start()
        across(level, 1, src).start()
        aside(level, 0, src).start()

    def cross(level, sign):
        copy(
            region(over_x, level, core), region(over_x, level, core), cross_sent.at[0, level],
            cross_got.at[0, level], (over_x, t),
        ).wait_recv()
        across(level, 2).start()
        aside(level, 1).start()
        copy(
            region(over_y, level, core), region(over_y, level, core), cross_sent.at[1, level],
            cross_got.at[1, level], (over_y, t),
        ).wait_recv()
        across(level, 3).start()
        aside(level, 2).start()

    def diagonal(level, sign):
        for kind in (2, 3):
            here = region(corner, level, core, kind - 2)
            copy(
                here, here, cross_sent.at[kind, level], cross_got.at[kind, level],
                (over_y if kind == 2 else over_x, t),
            ).wait_recv()
            aside(level, kind + 1).start()

    keep = pltpu.make_async_copy(own, region(p, z, core), local)
    keep.start()

    def at_distance(step, action):
        if step < 0 or step >= span:
            return
        if step == 0:
            action(z, 0)
            return

        @pl.when(z >= step)
        def _():
            action(z - step, -1)

        @pl.when(z + step < span)
        def _():
            action(z + step, 1)

    for step in range(span + 2):
        at_distance(step, column)
        at_distance(step - 1, cross)
        at_distance(step - 2, diagonal)

    keep.wait()
    for level in range(span):
        for kind in range(4):
            across(level, kind).wait_send()
        for kind in range(5):
            aside(level, kind).wait_send()
            aside(level, kind, which=1 - core).wait_recv()

        @pl.when((z >= level) & (z < span - 1))
        def _():
            along(level, 0).wait_send()

        @pl.when((z <= level) & (z > 0))
        def _():
            along(level, 1).wait_send()


def gather(inputs, cotangent, tensor_size, groups):
    tok, width = inputs.shape
    mine, span = width // BLOCK, tensor_size // 2
    vmem = pl.BlockSpec(memory_space=pltpu.VMEM)
    dma = pltpu.SemaphoreType.DMA
    return pl.pallas_call(
        functools.partial(gather_kernel, span),
        out_shape=jax.ShapeDtypeStruct((2, mine * tensor_size, tok * groups, BLOCK), BF16),
        in_specs=[vmem, vmem],
        out_specs=pl.BlockSpec(memory_space=pl.ANY),
        scratch_shapes=[
            pltpu.VMEM((2, mine, tok, BLOCK), BF16),
            dma(()),
            dma((2, span)), dma((4, span)), dma((5, span)),
            dma((span,)), dma((4, span)), dma((5, span)),
        ],
        compiler_params=pltpu.CompilerParams(
            collective_id=0, has_side_effects=True, vmem_limit_bytes=60 * 1024 * 1024
        ),
        name="gather",
    )(inputs, cotangent)


def finish_kernel(
    hidden_rows, feat_blocks, groups, span, grad_scale,
    lists, part, gg_hbm, gu_hbm, xt_hbm, ht_hbm, both_hbm,
    gx_ref, ggw_ref, guw_ref, gdw_ref,
    gg, gu, xt, ht, cot, dense, pair_in, pair_sum, peer_in, loads, pair_sems, sent, got,
):
    slots = lists.shape[1]
    rows = BLOCK // groups
    mine = feat_blocks // (2 * span)
    p, t = lax.axis_index("dp"), lax.axis_index("tensor")
    z, core = t // 2, t % 2
    other = t + 1 - 2 * core
    load_gg, load_xt, load_gu, load_ht, load_cot = [
        pltpu.make_async_copy(src, dst, loads.at[i])
        for i, (src, dst) in enumerate((
            (gg_hbm, gg), (xt_hbm, xt), (gu_hbm, gu), (ht_hbm, ht), (both_hbm.at[1], cot),
        ))
    ]

    barrier = pltpu.get_barrier_semaphore()

    def greet(device):
        pl.semaphore_signal(barrier, inc=1, device_id=device, device_id_type=pl.DeviceIdType.MESH)

    greet((p, other))
    for step in range(1, span):
        greet((p, (t + 2 * step) % (2 * span)))
    for load in (load_gg, load_xt, load_gu, load_ht, load_cot):
        load.start()
    pl.semaphore_wait(barrier, span)

    pair = pltpu.make_async_remote_copy(
        src_ref=part.at[1 - core], dst_ref=pair_in, send_sem=pair_sems.at[0], recv_sem=pair_sems.at[1],
        device_id=(p, other), device_id_type=pl.DeviceIdType.MESH,
    )
    pair.start()
    pair.wait_recv()

    def to_peer(step):
        to = (z + step) % span
        return pltpu.make_async_remote_copy(
            src_ref=pair_sum.at[to], dst_ref=peer_in.at[z], send_sem=sent.at[step],
            recv_sem=got.at[z], device_id=(p, to * 2 + core), device_id_type=pl.DeviceIdType.MESH,
        )

    for step in [*range(1, span), 0]:
        to = (z + step) % span

        @pl.loop(0, mine)
        def _(b):
            pair_sum[to, b] = (part[core, to, b].astype(F32) + pair_in[to, b].astype(F32)).astype(BF16)

        if step:
            to_peer(step).start()

    def all_products(left, right, count):
        @pl.loop(0, count // 2)
        def _(n):
            two = jnp.concatenate([right[2 * n], right[2 * n + 1]], axis=1)
            found = jnp.dot(left[...], two, preferred_element_type=F32) * grad_scale
            found = found.astype(BF16)
            per = left.shape[0] // rows
            for s in range(2):
                dense[pl.ds((2 * n + s) * per, per)] = found[:, s * BLOCK:(s + 1) * BLOCK].reshape(
                    per, rows, BLOCK
                )

    def pick_blocks(i, out, by_feat):
        @pl.loop(0, slots // SLOT_UNROLL)
        def _(n):
            for u in range(SLOT_UNROLL):
                k = n * SLOT_UNROLL + u
                e = lists[i, k]
                c = jnp.maximum(e, 0)
                d, h = c // hidden_rows, c % hidden_rows
                at = d * hidden_rows + h if by_feat else h * feat_blocks + d
                out[0, k] = dense[at]

    load_gg.wait()
    load_xt.wait()
    all_products(xt, gg, hidden_rows)
    pick_blocks(0, ggw_ref, False)
    load_gu.wait()
    all_products(xt, gu, hidden_rows)
    pick_blocks(1, guw_ref, False)
    load_ht.wait()
    load_cot.wait()
    all_products(ht, cot, feat_blocks)
    pick_blocks(2, gdw_ref, True)

    for step in range(1, span):
        at = (z + step) % span
        pltpu.make_async_remote_copy(
            src_ref=pair_sum.at[at], dst_ref=peer_in.at[at], send_sem=sent.at[step],
            recv_sem=got.at[at], device_id=(p, at * 2 + core), device_id_type=pl.DeviceIdType.MESH,
        ).wait_recv()
    for b in range(mine):
        total = pair_sum[z, b].astype(F32)
        for step in range(1, span):
            total = total + peer_in[(z + step) % span, b].astype(F32)
        gx_ref[:, b * BLOCK:(b + 1) * BLOCK] = total.astype(BF16)
    pair.wait_send()
    for step in range(1, span):
        to_peer(step).wait_send()


def finish(part, gg, gu, xt, ht, both, lists, tensor_size, groups):
    hidden_rows, tokens, _ = gg.shape
    feat_blocks = both.shape[1]
    slots = lists.shape[1]
    tok, rows, span = tokens // groups, BLOCK // groups, tensor_size // 2
    mine = feat_blocks // tensor_size
    smem = pl.BlockSpec(memory_space=pltpu.SMEM)
    vmem = pl.BlockSpec(memory_space=pltpu.VMEM)
    hbm = pl.BlockSpec(memory_space=pl.ANY)
    dma = pltpu.SemaphoreType.DMA
    grad = jax.ShapeDtypeStruct((1, slots, rows, BLOCK), BF16)
    bound = pltpu.VMEM((span, mine, tok, BLOCK), BF16)
    return pl.pallas_call(
        functools.partial(
            finish_kernel, hidden_rows, feat_blocks, groups, span, 1.0 / math.sqrt(tokens)
        ),
        out_shape=(jax.ShapeDtypeStruct((tok, mine * BLOCK), BF16), grad, grad, grad),
        in_specs=[smem, vmem, hbm, hbm, hbm, hbm, hbm],
        out_specs=[vmem] * 4,
        scratch_shapes=[
            pltpu.VMEM(gg.shape, BF16), pltpu.VMEM(gu.shape, BF16),
            pltpu.VMEM(xt.shape, BF16), pltpu.VMEM(ht.shape, BF16),
            pltpu.VMEM((feat_blocks, tokens, BLOCK), BF16),
            pltpu.VMEM((feat_blocks * hidden_rows, rows, BLOCK), BF16),
            bound, bound, bound,
            dma((5,)), dma((2,)), dma((span,)), dma((span,)),
        ],
        compiler_params=pltpu.CompilerParams(
            collective_id=1, has_side_effects=True, vmem_limit_bytes=60 * 1024 * 1024
        ),
        name="finish",
    )(lists, part, gg, gu, xt, ht, both)


def on_device(inputs, cotangent, gate_w, up_w, down_w, gate_list, up_list, down_list):
    tensor_size, groups = lax.axis_size("tensor"), lax.axis_size("dp")
    hidden_rows = FF // (BLOCK * tensor_size)
    slots = gate_list.shape[1]
    lists = jnp.concatenate([gate_list, up_list, down_list], axis=0)
    step = 2 * UNROLL
    length = (slots + hidden_rows + step - 1) // step * step
    tables, counts = pair_tables(lists, hidden_rows, length)

    both = gather(inputs, cotangent, tensor_size, groups)
    part, gg, gu, xt, ht = layer(
        both, gate_w, up_w, down_w, lists, tables, counts, hidden_rows, groups, tensor_size // 2
    )
    grad_x, *grads = finish(part, gg, gu, xt, ht, both, lists, tensor_size, groups)
    live = (lists >= 0)[:, None, :, None, None]
    return grad_x, *(jnp.where(live[i], grad, jnp.zeros_like(grad)) for i, grad in enumerate(grads))


def fits(mesh):
    return mesh.shape["dp"] == 4 and mesh.shape["tensor"] >= 4


def solution(mesh):
    return jax.shard_map(
        on_device if fits(mesh) else plain_on_device,
        mesh=mesh,
        in_specs=(
            P("dp", "tensor"),
            P("dp", "tensor"),
            P("tensor", None, None, None),
            P("tensor", None, None, None),
            P("tensor", None, None, None),
            P("tensor", None),
            P("tensor", None),
            P("tensor", None),
        ),
        out_specs=(
            P("dp", "tensor"),
            P("tensor", None, "dp", None),
            P("tensor", None, "dp", None),
            P("tensor", None, "dp", None),
        ),
        check_vma=False,
    )
```
